32 devices in a mesh: wide: 4 (over y, core), narrow: 4 (over z), net: 2 (over x).
Axes of the slice: x: 2, y: 2, z: 4, core: 2. Of those that a mesh axis runs over, the one named last changes fastest.
Arguments:
- fields: float32 [4, 16, 16, 1024], P(None, 'net', 'wide', 'narrow'), may hold values from -7.5 to 7.5
- conv1_weight: bfloat16 [27, 32, 4], replicated, may hold values from -0.625 to 0.625
- conv1_bias: float32 [32], replicated, may hold values from -6 to 6
- conv2_weight: bfloat16 [27, 6, 32], replicated, may hold values from -0.21875 to 0.21875
Outputs:
- advanced: float32 [4, 16, 16, 1024], P(None, 'net', 'wide', 'narrow')
The draws below stay inside these ranges and needn't reach their ends.
All inputs are finite; a program needn't handle non-finite values.
Results may differ from the reference program's by a relative error of at most 0.0028.
Values may be sent and summed in bfloat16 or wider, within the bound.
A program may use at most 64 MiB of HBM per device.

```python
import jax
import jax.numpy as jnp
from jax import lax

FIELDS = 4
STRESS = 6
HIDDEN_SIZE = 32
NX = 16
NY = 1024
NZ = 16


def level_of(key, extent, cuts, low, largest):
    level, own = 1.0, jax.random.fold_in(key, 6)
    for axis_at, shards_of in cuts:
        draws = jnp.exp(jax.random.uniform(jax.random.fold_in(own, axis_at), (shards_of,), jnp.float32, low / len(cuts), largest / len(cuts)))
        level = level * jnp.repeat(draws, extent[axis_at] // shards_of).reshape([-1 if axis == axis_at else 1 for axis in range(len(extent))])
    return level


def bell_draw(own_key, dims, scale, reach, shards=(), kind=jnp.bfloat16):
    factor_of = level_of(own_key, dims, shards, -0.22, 0.18) if shards else 1.0
    values = jax.random.normal(own_key, dims, jnp.float32) * scale * factor_of
    return jnp.minimum(jnp.maximum(values, -reach), reach).astype(kind)


def setup_inputs(seed: int = 0) -> dict:
    seeds = jax.random.split(jax.random.key(seed), 5)
    fields = bell_draw(seeds[0], (FIELDS, NZ, NX, NY), 3.0, 7.5, ((1, 2), (2, 4), (3, 4)), jnp.float32)
    conv1_weight = jnp.clip(jax.random.uniform(seeds[1], (27, HIDDEN_SIZE, FIELDS), jnp.float32, -0.625, 0.625), -0.625, 0.625).astype(jnp.bfloat16)
    conv1_bias = bell_draw(seeds[2], (HIDDEN_SIZE,), 2.0, 6.0, (), jnp.float32)
    conv2_weight = jnp.clip(jax.random.uniform(seeds[3], (27, STRESS, HIDDEN_SIZE), jnp.float32, -0.21875, 0.21875), -0.21875, 0.21875).astype(jnp.bfloat16)
    return {"fields": fields, "conv1_weight": conv1_weight, "conv1_bias": conv1_bias, "conv2_weight": conv2_weight}


time_step = 0.2
viscosity = 0.05


def neighbour(field, offset, axis):
    return jnp.roll(field, -offset, axis=axis)


def coarsen(fields):
    channels, deep_cells, row_cells, col_cells = fields.shape
    grouped = fields.reshape(channels, deep_cells // 2, 2, row_cells // 2, 2, col_cells // 2, 2)
    return jnp.mean(grouped, axis=(2, 4, 6))


def convolve(inputs, weights):
    padded = jnp.pad(inputs.astype(jnp.float32), ((0, 0), (1, 1), (1, 1), (1, 1)), mode="wrap")
    outputs = weights.shape[1]
    channels = weights.shape[2]
    kernel = weights.astype(jnp.float32).reshape(3, 3, 3, outputs, channels).transpose(3, 4, 0, 1, 2)
    result = lax.conv_general_dilated(padded[None], kernel, (1, 1, 1), "VALID", dimension_numbers=("NCDHW", "OIDHW", "NCDHW"), precision=lax.Precision.HIGHEST, preferred_element_type=jnp.float32)
    return result[0]


def derivative(field, axis):
    return (neighbour(field, 1, axis) - neighbour(field, -1, axis)) * 0.25


def divergence(stress):
    values = stress.astype(jnp.float32)
    force_x = derivative(values[0], 1) + derivative(values[3], 2) + derivative(values[4], 0)
    force_y = derivative(values[3], 1) + derivative(values[1], 2) + derivative(values[5], 0)
    force_z = derivative(values[4], 1) + derivative(values[5], 2) + derivative(values[2], 0)
    return jnp.stack([force_x, force_y, force_z])


def upsample(field):
    return jnp.repeat(jnp.repeat(jnp.repeat(field, 2, 0), 2, 1), 2, 2)


def tendency(state, forcing):
    results = []
    for index in range(state.shape[0]):
        field = state[index]
        grad_z = (neighbour(field, 1, 0) - neighbour(field, -1, 0)) * 0.5
        grad_x = (neighbour(field, 1, 1) - neighbour(field, -1, 1)) * 0.5
        grad_y = (neighbour(field, 1, 2) - neighbour(field, -1, 2)) * 0.5
        spread = neighbour(field, 1, 0) + neighbour(field, -1, 0) + neighbour(field, 1, 1) + neighbour(field, -1, 1) + neighbour(field, 1, 2) + neighbour(field, -1, 2) - 6.0 * field
        change = viscosity * spread - (state[0] * grad_x + state[1] * grad_y + state[2] * grad_z)
        if index < 3:
            change = change + upsample(forcing[index])
        results.append(change)
    return jnp.stack(results)


def reference(fields, conv1_weight, conv1_bias, conv2_weight):
    def rate(state):
        coarse = lax.optimization_barrier(coarsen(state).astype(jnp.bfloat16))
        hidden = jax.nn.gelu(convolve(coarse, conv1_weight) + conv1_bias[:, None, None, None], approximate=True)
        hidden = lax.optimization_barrier(hidden.astype(jnp.bfloat16))
        stress = lax.optimization_barrier(convolve(hidden, conv2_weight).astype(jnp.bfloat16))
        return tendency(state, divergence(stress))

    section_one = fields + time_step * rate(fields)
    section_two = 0.75 * fields + 0.25 * (section_one + time_step * rate(section_one))
    return fields / 3.0 + (2.0 / 3.0) * (section_two + time_step * rate(section_two))
```

```python
import functools
import math

import jax
import jax.numpy as jnp
import numpy as np
from jax import lax
from jax.experimental import pallas as pl
from jax.experimental.pallas import tpu as pltpu
from jax.sharding import PartitionSpec as P

MESH = pl.DeviceIdType.MESH
TIME_STEP = 0.2
VISCOSITY = 0.05
EDGE = 128


def gather_kernel(nets, wides, narrows, own_ref, main_ref, edge_ref, after, before, packed,
                  y_send, y_recv, main_send, main_recv, edge_send, edge_recv, local_sem):
    net, wide, narrow = lax.axis_index("net"), lax.axis_index("wide"), lax.axis_index("narrow")
    up, down = lax.rem(narrow + 1, narrows), lax.rem(narrow + narrows - 1, narrows)
    length = own_ref.shape[1]
    offsets = [(dn, dw) for dn in range(nets) for dw in range(wides) if (dn, dw) != (0, 0)]

    def device(n, w, k):
        return {"net": n, "wide": w, "narrow": k}

    def target(dn, dw):
        return device(lax.rem(net + nets - dn, nets), lax.rem(wide + wides - dw, wides), narrow)

    barrier = pltpu.get_barrier_semaphore()
    for k in (up, down):
        pl.semaphore_signal(barrier, inc=1, device_id=device(net, wide, k), device_id_type=MESH)
    for dn, dw in offsets:
        pl.semaphore_signal(barrier, inc=1, device_id=target(dn, dw), device_id_type=MESH)
    pl.semaphore_wait(barrier, 2 + len(offsets))

    def remote(src, dst, send, recv, where):
        return pltpu.make_async_remote_copy(
            src_ref=src, dst_ref=dst, send_sem=send, recv_sem=recv, device_id=where, device_id_type=MESH
        )

    to_down = remote(own_ref.at[:, pl.ds(0, EDGE)], after, y_send.at[0], y_recv.at[0], device(net, wide, down))
    to_up = remote(own_ref.at[:, pl.ds(length - EDGE, EDGE)], before, y_send.at[1], y_recv.at[1], device(net, wide, up))
    to_down.start()
    to_up.start()
    mains = []
    for dn, dw in offsets:
        slot = dn * wides + dw
        mains.append(remote(own_ref, main_ref.at[slot], main_send.at[slot], main_recv.at[slot], target(dn, dw)))
        mains[-1].start()
    own_main = pltpu.make_async_copy(own_ref, main_ref.at[0], local_sem.at[0])
    own_main.start()
    to_down.wait()
    to_up.wait()
    lane = lax.broadcasted_iota(jnp.int32, after.shape, 1)
    packed[...] = jnp.where(
        lane < EDGE // 2, after[...].astype(jnp.float32), before[...].astype(jnp.float32)
    ).astype(packed.dtype)
    edges = []
    for dn, dw in offsets:
        slot = dn * wides + dw
        edges.append(remote(packed, edge_ref.at[slot], edge_send.at[slot], edge_recv.at[slot], target(dn, dw)))
        edges[-1].start()
    own_edge = pltpu.make_async_copy(packed, edge_ref.at[0], local_sem.at[1])
    own_edge.start()
    for copy in mains + edges + [own_main, own_edge]:
        copy.wait()


def gather(own, nets, wides, narrows):
    rows, length = own.shape
    slots = nets * wides
    return pl.pallas_call(
        functools.partial(gather_kernel, nets, wides, narrows),
        out_shape=[
            jax.ShapeDtypeStruct((slots, rows, length), own.dtype),
            jax.ShapeDtypeStruct((slots, rows, EDGE), own.dtype),
        ],
        in_specs=[pl.BlockSpec(memory_space=pltpu.VMEM)],
        out_specs=[pl.BlockSpec(memory_space=pl.ANY)] * 2,
        scratch_shapes=[
            pltpu.VMEM((rows, EDGE), own.dtype),
            pltpu.VMEM((rows, EDGE), own.dtype),
            pltpu.VMEM((rows, EDGE), own.dtype),
            pltpu.SemaphoreType.DMA((2,)),
            pltpu.SemaphoreType.DMA((2,)),
            pltpu.SemaphoreType.DMA((slots,)),
            pltpu.SemaphoreType.DMA((slots,)),
            pltpu.SemaphoreType.DMA((slots,)),
            pltpu.SemaphoreType.DMA((slots,)),
            pltpu.SemaphoreType.DMA((2,)),
        ],
        compiler_params=pltpu.CompilerParams(collective_id=0, has_side_effects=True),
    )(own)


def shifted(values, offset, axis):
    return pltpu.roll(values, (-offset) % values.shape[axis], axis)


def two_parts(values):
    high = values.astype(jnp.bfloat16)
    low = (values - high.astype(jnp.float32)).astype(jnp.bfloat16)
    return high, low


def gelu(x):
    inner = x * (0.7978845608028654 + 0.035677408136300125 * (x * x))
    half = 0.5 * x
    return half + half * jnp.tanh(inner)


def step_kernel(nets, wides, main_ref, edge_ref, own_ref, w1_ref, bias_ref, w2_ref, pool_ref, spread_ref,
                out_ref, base, state, thin, taps, stress, flux, force, mains, edges, arrived):
    fields, xs, depth, lanes = own_ref.shape
    big_x, big_z, ring = base.shape[1:]
    coarse_x = big_x // 2
    coarse_ring = pool_ref.shape[1]
    block = fields * big_z
    parts = 6 * big_z
    part_x = thin.shape[0] // block
    stage = mains.shape[0]
    unroll = 2 if big_z <= 16 else 1

    for begin in range(0, nets * wides, stage):
        copies = [
            pltpu.make_async_copy(main_ref.at[pl.ds(begin, stage)], mains, arrived.at[0]),
            pltpu.make_async_copy(edge_ref.at[pl.ds(begin, stage)], edges, arrived.at[1]),
        ]
        for copy in copies:
            copy.start()
        for copy in copies:
            copy.wait()
        for i in range(stage):
            dn, dw = divmod(begin + i, wides)
            x_at, z_at = pl.ds(dw * xs, xs), pl.ds(dn * depth, depth)
            if begin + i == 0:
                base[:, x_at, z_at, pl.ds(0, lanes)] = own_ref[...]
            else:
                base[:, x_at, z_at, pl.ds(0, lanes)] = (
                    mains[i].astype(jnp.float32).reshape(fields, xs, depth, lanes)
                )
            base[:, x_at, z_at, pl.ds(lanes, EDGE)] = (
                edges[i].astype(jnp.float32).reshape(fields, xs, depth, EDGE)
            )

    def wrapped(i, size):
        return lax.rem(i + size, size)

    def forces(src):
        for chunk in range(0, coarse_x, part_x):
            @pl.loop(0, part_x, unroll=unroll)
            def _(i):
                x = chunk + i
                for c in range(fields):
                    both = src[c, 2 * x] + src[c, 2 * x + 1]
                    both = both + shifted(both, 1, 0)
                    high, low = two_parts(both)
                    at = pl.ds(pl.multiple_of(i * block + c * big_z, big_z), big_z)
                    thin[at, pl.ds(0, ring)] = high
                    thin[at, pl.ds(ring, ring)] = low

            coarse = jnp.dot(thin[...], pool_ref[...], preferred_element_type=jnp.float32)
            for dy in range(3):
                moved = (coarse if dy == 1 else shifted(coarse, dy - 1, 1)).astype(jnp.bfloat16)
                taps[pl.ds(chunk + 1, part_x), dy] = moved.reshape(part_x, block, coarse_ring)

        taps[0] = taps[coarse_x]
        taps[coarse_x + 1] = taps[1]
        stress[...] = jnp.zeros_like(stress)

        @pl.loop(0, coarse_x, unroll=unroll)
        def _(x):
            around = taps[pl.ds(x, 3)].reshape(9 * block, coarse_ring)
            hidden = jnp.dot(w1_ref[...], around, preferred_element_type=jnp.float32) + bias_ref[...]
            hidden = gelu(hidden)
            wide_hidden = jnp.concatenate(
                [(hidden if dy == 1 else shifted(hidden, dy - 1, 1)).astype(jnp.bfloat16) for dy in range(3)], axis=0
            )
            partial = jnp.dot(w2_ref[...], wide_hidden, preferred_element_type=jnp.float32)
            for dx in range(3):
                at = wrapped(x + 1 - dx, coarse_x)
                stress[at] += partial[dx * parts : (dx + 1) * parts].reshape(6, big_z, coarse_ring)

        @pl.loop(0, coarse_x, unroll=unroll)
        def _(x):
            stress[x] = stress[x].astype(jnp.bfloat16).astype(jnp.float32)

        for chunk in range(0, coarse_x, part_x):
            @pl.loop(0, part_x, unroll=unroll)
            def _(i):
                x = chunk + i
                here = [stress[x, c] for c in range(6)]
                ahead, behind = wrapped(x + 1, coarse_x), wrapped(x - 1, coarse_x)
                for axis, (in_x, in_y, in_z) in enumerate(((0, 3, 4), (3, 1, 5), (4, 5, 2))):
                    total = stress[ahead, in_x] - stress[behind, in_x]
                    total = total + shifted(here[in_y], 1, 1) - shifted(here[in_y], -1, 1)
                    total = total + shifted(here[in_z], 2, 0) - shifted(here[in_z], -2, 0)
                    high, low = two_parts(0.25 * total)
                    at = pl.ds(pl.multiple_of((i * 3 + axis) * big_z, big_z), big_z)
                    flux[at, pl.ds(0, coarse_ring)] = high
                    flux[at, pl.ds(coarse_ring, coarse_ring)] = low

            fine = jnp.dot(flux[...], spread_ref[...], preferred_element_type=jnp.float32)
            force[pl.ds(chunk, part_x)] = fine.reshape(part_x, 3, big_z, ring)

    def rates(src, x, give):
        ahead, behind = wrapped(x + 1, big_x), wrapped(x - 1, big_x)
        half = [0.5 * src[c, x] for c in range(3)]
        u, v, w = half
        plus = [VISCOSITY - h for h in half]
        minus = [VISCOSITY + h for h in half]
        for c in range(fields):
            q = src[c, x]
            rate = plus[0] * src[c, ahead] + minus[0] * src[c, behind]
            rate = rate + plus[1] * shifted(q, 1, 1) + minus[1] * shifted(q, -1, 1)
            rate = rate + plus[2] * shifted(q, 1, 0) + minus[2] * shifted(q, -1, 0)
            rate = rate - (6.0 * VISCOSITY) * q
            if c < 3:
                rate = rate + force[x // 2, c]
            give(c, q, rate)

    forces(base)

    @pl.loop(0, big_x, unroll=unroll)
    def _(x):
        def give(c, q, rate):
            state[c, x] = q + TIME_STEP * rate

        rates(base, x, give)

    forces(state)

    @pl.loop(0, big_x, unroll=unroll)
    def _(x):
        def give(c, q, rate):
            base[c, x] = 0.75 * base[c, x] + 0.25 * (q + TIME_STEP * rate)

        rates(state, x, give)

    forces(base)

    for x in range(xs):
        def give(c, q, rate):
            moved = (q + TIME_STEP * rate)[:depth, :lanes]
            out_ref[c, x] = own_ref[c, x] * (1.0 / 3.0) + (2.0 / 3.0) * moved

        rates(base, x, give)


def step(main, edge, own, w1, bias, w2, pool, spread, nets, wides):
    fields, xs, depth, lanes = own.shape
    big_x, big_z, ring = xs * wides, depth * nets, lanes + EDGE
    coarse_x, coarse_ring = big_x // 2, lanes // 2 + EDGE
    part_x = math.gcd(coarse_x, max(1, 512 // (fields * big_z)))
    stage = math.gcd(nets * wides, 8)
    return pl.pallas_call(
        functools.partial(step_kernel, nets, wides),
        out_shape=jax.ShapeDtypeStruct(own.shape, jnp.float32),
        in_specs=[pl.BlockSpec(memory_space=pl.ANY)] * 2 + [pl.BlockSpec(memory_space=pltpu.VMEM)] * 6,
        out_specs=pl.BlockSpec(memory_space=pltpu.VMEM),
        scratch_shapes=[
            pltpu.VMEM((fields, big_x, big_z, ring), jnp.float32),
            pltpu.VMEM((fields, big_x, big_z, ring), jnp.float32),
            pltpu.VMEM((part_x * fields * big_z, 2 * ring), jnp.bfloat16),
            pltpu.VMEM((coarse_x + 2, 3, fields * big_z, coarse_ring), jnp.bfloat16),
            pltpu.VMEM((coarse_x, 6, big_z, coarse_ring), jnp.float32),
            pltpu.VMEM((part_x * 3 * big_z, 2 * coarse_ring), jnp.bfloat16),
            pltpu.VMEM((coarse_x, 3, big_z, ring), jnp.float32),
            pltpu.VMEM((stage, *main.shape[1:]), main.dtype),
            pltpu.VMEM((stage, *edge.shape[1:]), edge.dtype),
            pltpu.SemaphoreType.DMA((2,)),
        ],
        compiler_params=pltpu.CompilerParams(vmem_limit_bytes=60 * 1024 * 1024),
    )(main, edge, own, w1, bias, w2, pool, spread)


def constants(lanes, big_z):
    ring, coarse_ring, coarse_z = lanes + EDGE, lanes // 2 + EDGE, big_z // 2
    covers = np.zeros((ring, coarse_ring), np.float32)
    for m in range(coarse_ring):
        if m < lanes // 2 + EDGE // 4:
            first = 2 * m
        elif m >= coarse_ring - EDGE // 4:
            first = ring - 2 * (coarse_ring - m)
        else:
            continue
        covers[first : first + 2, m] = 1.0
    pool = np.concatenate([covers, covers], 0) * 0.125
    spread = np.concatenate([covers.T, covers.T], 0)
    first = np.zeros((coarse_z, big_z, 3), np.float32)
    second = np.zeros((big_z, coarse_z, 3), np.float32)
    for dz in range(3):
        for z in range(coarse_z):
            first[z, 2 * ((z + dz - 1) % coarse_z), dz] = 1.0
        for z in range(big_z):
            second[z, (z // 2 + dz - 1) % coarse_z, dz] = 1.0
    return [jnp.asarray(a, jnp.bfloat16) for a in (pool, spread, first, second)]


def per_device(nets, wides, narrows, fields, conv1_weight, conv1_bias, conv2_weight):
    count, depth, xs, lanes = fields.shape
    big_z = depth * nets
    pool, spread, first, second = constants(lanes, big_z)
    own = fields.transpose(0, 2, 1, 3)
    main, edge = gather(own.astype(jnp.bfloat16).reshape(-1, lanes), nets, wides, narrows)
    hidden, channels = conv1_weight.shape[1:]
    parts = conv2_weight.shape[1]
    w1 = jnp.einsum("dxyoc,pqd->poxycq", conv1_weight.reshape(3, 3, 3, hidden, channels), first)
    w1 = w1.reshape(big_z // 2 * hidden, 9 * channels * big_z)
    w2 = jnp.einsum("dxysh,rqd->xsryqh", conv2_weight.reshape(3, 3, 3, parts, hidden), second)
    w2 = w2.reshape(3 * parts * big_z, 3 * big_z // 2 * hidden)
    bias = jnp.tile(conv1_bias, big_z // 2)[:, None]
    moved = step(main, edge, own, w1, bias, w2, pool, spread, nets, wides)
    return moved.transpose(0, 2, 1, 3)


def solution(mesh):
    in_specs = (P(None, "net", "wide", "narrow"), P(), P(), P())
    out_specs = P(None, "net", "wide", "narrow")
    sizes = (mesh.shape["net"], mesh.shape["wide"], mesh.shape["narrow"])
    return jax.shard_map(
        functools.partial(per_device, *sizes), mesh=mesh, in_specs=in_specs, out_specs=out_specs, check_vma=False
    )
```

```python
import functools
import math

import jax
import jax.numpy as jnp
import numpy as np
from jax import lax
from jax.experimental import pallas as pl
from jax.experimental.pallas import tpu as pltpu
from jax.sharding import PartitionSpec as P

MESH = pl.DeviceIdType.MESH
TIME_STEP = 0.2
VISCOSITY = 0.05
EDGE = 128


def gather_kernel(nets, wides, narrows, own_ref, main_ref, edge_ref, after, before, packed,
                  y_send, y_recv, main_send, main_recv, edge_send, edge_recv, local_sem):
    net, wide, narrow = lax.axis_index("net"), lax.axis_index("wide"), lax.axis_index("narrow")
    up, down = lax.rem(narrow + 1, narrows), lax.rem(narrow + narrows - 1, narrows)
    length = own_ref.shape[1]
    offsets = [(dn, dw) for dn in range(nets) for dw in range(wides) if (dn, dw) != (0, 0)]

    def device(n, w, k):
        return {"net": n, "wide": w, "narrow": k}

    def target(dn, dw):
        return device(lax.rem(net + nets - dn, nets), lax.rem(wide + wides - dw, wides), narrow)

    barrier = pltpu.get_barrier_semaphore()
    for k in (up, down):
        pl.semaphore_signal(barrier, inc=1, device_id=device(net, wide, k), device_id_type=MESH)
    for dn, dw in offsets:
        pl.semaphore_signal(barrier, inc=1, device_id=target(dn, dw), device_id_type=MESH)
    pl.semaphore_wait(barrier, 2 + len(offsets))

    def remote(src, dst, send, recv, where):
        return pltpu.make_async_remote_copy(
            src_ref=src, dst_ref=dst, send_sem=send, recv_sem=recv, device_id=where, device_id_type=MESH
        )

    to_down = remote(own_ref.at[:, pl.ds(0, EDGE)], after, y_send.at[0], y_recv.at[0], device(net, wide, down))
    to_up = remote(own_ref.at[:, pl.ds(length - EDGE, EDGE)], before, y_send.at[1], y_recv.at[1], device(net, wide, up))
    to_down.start()
    to_up.start()
    mains = []
    for dn, dw in offsets:
        slot = dn * wides + dw
        mains.append(remote(own_ref, main_ref.at[slot], main_send.at[slot], main_recv.at[slot], target(dn, dw)))
        mains[-1].start()
    own_main = pltpu.make_async_copy(own_ref, main_ref.at[0], local_sem.at[0])
    own_main.start()
    to_down.wait()
    to_up.wait()
    lane = lax.broadcasted_iota(jnp.int32, after.shape, 1)
    packed[...] = jnp.where(
        lane < EDGE // 2, after[...].astype(jnp.float32), before[...].astype(jnp.float32)
    ).astype(packed.dtype)
    edges = []
    for dn, dw in offsets:
        slot = dn * wides + dw
        edges.append(remote(packed, edge_ref.at[slot], edge_send.at[slot], edge_recv.at[slot], target(dn, dw)))
        edges[-1].start()
    own_edge = pltpu.make_async_copy(packed, edge_ref.at[0], local_sem.at[1])
    own_edge.start()
    for copy in mains + edges + [own_main, own_edge]:
        copy.wait()


def gather(own, nets, wides, narrows):
    rows, length = own.shape
    slots = nets * wides
    return pl.pallas_call(
        functools.partial(gather_kernel, nets, wides, narrows),
        out_shape=[
            jax.ShapeDtypeStruct((slots, rows, length), own.dtype),
            jax.ShapeDtypeStruct((slots, rows, EDGE), own.dtype),
        ],
        in_specs=[pl.BlockSpec(memory_space=pltpu.VMEM)],
        out_specs=[pl.BlockSpec(memory_space=pl.ANY)] * 2,
        scratch_shapes=[
            pltpu.VMEM((rows, EDGE), own.dtype),
            pltpu.VMEM((rows, EDGE), own.dtype),
            pltpu.VMEM((rows, EDGE), own.dtype),
            pltpu.SemaphoreType.DMA((2,)),
            pltpu.SemaphoreType.DMA((2,)),
            pltpu.SemaphoreType.DMA((slots,)),
            pltpu.SemaphoreType.DMA((slots,)),
            pltpu.SemaphoreType.DMA((slots,)),
            pltpu.SemaphoreType.DMA((slots,)),
            pltpu.SemaphoreType.DMA((2,)),
        ],
        compiler_params=pltpu.CompilerParams(collective_id=0, has_side_effects=True),
    )(own)


def shifted(values, offset, axis):
    return pltpu.roll(values, (-offset) % values.shape[axis], axis)


def two_parts(values):
    high = values.astype(jnp.bfloat16)
    low = (values - high.astype(jnp.float32)).astype(jnp.bfloat16)
    return high, low


def gelu(x):
    inner = x * (0.7978845608028654 + 0.035677408136300125 * (x * x))
    half = 0.5 * x
    return half + half * jnp.tanh(inner)


def step_kernel(nets, wides, main_ref, edge_ref, own_ref, w1_ref, bias_ref, w2_ref, pool_ref, spread_ref,
                out_ref, base, state, thin, taps, wide_hidden, partial, turned, upper, force, mains, edges, arrived):
    fields, xs, depth, lanes = own_ref.shape
    big_x, big_z, ring = base.shape[1:]
    coarse_x, coarse_z = big_x // 2, big_z // 2
    coarse_ring = pool_ref.shape[0]
    block = fields * big_z
    part_x = thin.shape[0] // block
    stage = mains.shape[0]
    unroll = 2 if big_z <= 16 else 1
    variants, window = w1_ref.shape[0], w1_ref.shape[2]
    pad = (taps.shape[2] - coarse_x * block) // 2
    channels = w2_ref.shape[1]
    width = w2_ref.shape[2] // 3
    batch = wide_hidden.shape[0]
    together = max(1, 128 // width)

    for begin in range(0, nets * wides, stage):
        copies = [
            pltpu.make_async_copy(main_ref.at[pl.ds(begin, stage)], mains, arrived.at[0]),
            pltpu.make_async_copy(edge_ref.at[pl.ds(begin, stage)], edges, arrived.at[1]),
        ]
        for copy in copies:
            copy.start()
        for copy in copies:
            copy.wait()
        for i in range(stage):
            dn, dw = divmod(begin + i, wides)
            x_at, z_at = pl.ds(dw * xs, xs), pl.ds(dn * depth, depth)
            if begin + i == 0:
                base[:, x_at, z_at, pl.ds(0, lanes)] = own_ref[...]
            else:
                base[:, x_at, z_at, pl.ds(0, lanes)] = (
                    mains[i].astype(jnp.float32).reshape(fields, xs, depth, lanes)
                )
            base[:, x_at, z_at, pl.ds(lanes, EDGE)] = (
                edges[i].astype(jnp.float32).reshape(fields, xs, depth, EDGE)
            )

    def each(count, body):
        if count == 1:
            body(0)
        else:
            pl.loop(0, count)(body)

    def wrapped(i, size):
        return (i + size) % size if isinstance(i, int) else lax.rem(i + size, size)

    def forces(src):
        @functools.partial(each, coarse_x // part_x)
        def _(turn):
            chunk = turn * part_x

            @pl.loop(0, part_x, unroll=unroll)
            def _(i):
                x = chunk + i
                for c in range(fields):
                    both = src[c, 2 * x] + src[c, 2 * x + 1]
                    both = both + shifted(both, 1, 0)
                    high, low = two_parts(both)
                    at = pl.ds(pl.multiple_of(i * block + c * big_z, big_z), big_z)
                    thin[at, pl.ds(0, ring)] = high
                    thin[at, pl.ds(ring, ring)] = low

            coarse = lax.dot_general(
                pool_ref[...], thin[...], (((1,), (1,)), ((), ())), preferred_element_type=jnp.float32
            )
            for dy in range(3):
                moved = (coarse if dy == 1 else shifted(coarse, dy - 1, 0)).astype(jnp.bfloat16)
                at = pl.multiple_of(pad + chunk * block, 128)
                taps[dy, :, pl.ds(at, part_x * block)] = moved

        span = coarse_x * block
        taps[:, :, pl.ds(0, pad)] = taps[:, :, pl.ds(span, pad)]
        taps[:, :, pl.ds(pad + span, pad)] = taps[:, :, pl.ds(pad, pad)]

        if batch < coarse_x:
            partial[...] = jnp.zeros_like(partial)

        @functools.partial(each, coarse_x // batch)
        def _(turn):
            begin = turn * batch
            for variant in range(variants):
                mine = list(range(variant, batch, variants))
                rows = []
                for x in mine:
                    at = pl.multiple_of(begin * block + (pad + (x - 1) * block) // 128 * 128, 128)
                    rows.append(jnp.concatenate([taps[dy, :, pl.ds(at, window)] for dy in range(3)], axis=1))
                around = jnp.concatenate(rows, axis=0)
                weight = w1_ref[variant].reshape(3 * window, channels)
                hidden = jnp.dot(around, weight, preferred_element_type=jnp.float32) + bias_ref[...]
                hidden = gelu(hidden)
                for i, x in enumerate(mine):
                    here = hidden[i * coarse_ring : (i + 1) * coarse_ring]
                    for dy in range(3):
                        moved = (here if dy == 1 else shifted(here, dy - 1, 0)).astype(jnp.bfloat16)
                        wide_hidden[x, :, pl.ds(dy * channels, channels)] = moved
            found = jnp.dot(
                wide_hidden[...].reshape(batch * coarse_ring, 3 * channels),
                w2_ref[...].reshape(3 * channels, 3 * width),
                preferred_element_type=jnp.float32,
            )
            found = found.reshape(batch, coarse_ring, 3 * width)
            for i in range(batch):
                if batch == coarse_x:
                    total = found[(i - 1) % coarse_x, :, :width] + found[i, :, width : 2 * width]
                    partial[i] = total + found[(i + 1) % coarse_x, :, 2 * width :]
                else:
                    for dx in range(3):
                        partial[wrapped(begin + i + 1 - dx, coarse_x)] += found[i, :, dx * width : (dx + 1) * width]

        def turn_over(x):
            totals = [partial[x + i] for i in range(together)]
            total = jnp.concatenate(totals, axis=1) if together > 1 else totals[0]
            at = x * width if isinstance(x, int) else pl.multiple_of(x * width, width)
            turned[pl.ds(at, together * width), :] = total.T.astype(jnp.bfloat16)

        if batch == coarse_x:
            for x in range(0, coarse_x, together):
                turn_over(x)
        else:
            pl.loop(0, coarse_x // together)(lambda i: turn_over(i * together))

        @functools.partial(each, coarse_x // batch)
        def _(turn):
            begin = turn * batch
            at = pl.multiple_of(begin * width, batch * width)
            fine = jnp.dot(
                turned[pl.ds(at, batch * width), :], spread_ref[...], preferred_element_type=jnp.float32
            )
            upper[pl.ds(begin, batch)] = fine.reshape(batch, width, ring)

        @pl.loop(0, coarse_x, unroll=unroll)
        def _(x):
            ahead, behind = wrapped(x + 1, coarse_x), wrapped(x - 1, coarse_x)

            def part(at, component):
                return upper[at, pl.ds(component * coarse_z, coarse_z)]

            for axis, (in_x, in_y, in_z) in enumerate(((0, 3, 4), (3, 1, 5), (4, 5, 2))):
                along_y, along_z = part(x, in_y), part(x, in_z)
                total = part(ahead, in_x) - part(behind, in_x)
                total = total + shifted(along_y, 2, 1) - shifted(along_y, -2, 1)
                total = 0.25 * (total + shifted(along_z, 1, 0) - shifted(along_z, -1, 0))
                force[x, axis] = jnp.broadcast_to(total[:, None], (coarse_z, 2, ring)).reshape(big_z, ring)

    def rates(src, x, give):
        ahead, behind = wrapped(x + 1, big_x), wrapped(x - 1, big_x)
        half = [0.5 * src[c, x] for c in range(3)]
        u, v, w = half
        plus = [VISCOSITY - h for h in half]
        minus = [VISCOSITY + h for h in half]
        for c in range(fields):
            q = src[c, x]
            rate = plus[0] * src[c, ahead] + minus[0] * src[c, behind]
            rate = rate + plus[1] * shifted(q, 1, 1) + minus[1] * shifted(q, -1, 1)
            rate = rate + plus[2] * shifted(q, 1, 0) + minus[2] * shifted(q, -1, 0)
            rate = rate - (6.0 * VISCOSITY) * q
            if c < 3:
                rate = rate + force[x // 2, c]
            give(c, q, rate)

    forces(base)

    @pl.loop(0, big_x, unroll=unroll)
    def _(x):
        def give(c, q, rate):
            state[c, x] = q + TIME_STEP * rate

        rates(base, x, give)

    forces(state)

    @pl.loop(0, big_x, unroll=unroll)
    def _(x):
        def give(c, q, rate):
            base[c, x] = 0.75 * base[c, x] + 0.25 * (q + TIME_STEP * rate)

        rates(state, x, give)

    forces(base)

    for x in range(xs):
        def give(c, q, rate):
            moved = (q + TIME_STEP * rate)[:depth, :lanes]
            out_ref[c, x] = own_ref[c, x] * (1.0 / 3.0) + (2.0 / 3.0) * moved

        rates(base, x, give)


def step(main, edge, own, w1, bias, w2, pool, spread, nets, wides):
    fields, xs, depth, lanes = own.shape
    big_x, big_z, ring = xs * wides, depth * nets, lanes + EDGE
    coarse_x, coarse_ring = big_x // 2, pool.shape[0]
    block = fields * big_z
    part_x = math.gcd(coarse_x, max(1, 512 // block))
    stage = math.gcd(nets * wides, 8)
    batch = math.gcd(coarse_x, 8 if block < 128 else 1)
    channels, width = w2.shape[1], w2.shape[2] // 3
    return pl.pallas_call(
        functools.partial(step_kernel, nets, wides),
        out_shape=jax.ShapeDtypeStruct(own.shape, jnp.float32),
        in_specs=[pl.BlockSpec(memory_space=pl.ANY)] * 2 + [pl.BlockSpec(memory_space=pltpu.VMEM)] * 6,
        out_specs=pl.BlockSpec(memory_space=pltpu.VMEM),
        scratch_shapes=[
            pltpu.VMEM((fields, big_x, big_z, ring), jnp.float32),
            pltpu.VMEM((fields, big_x, big_z, ring), jnp.float32),
            pltpu.VMEM((part_x * block, 2 * ring), jnp.bfloat16),
            pltpu.VMEM((3, coarse_ring, coarse_x * block + 2 * max(128, block)), jnp.bfloat16),
            pltpu.VMEM((batch, coarse_ring, 3 * channels), jnp.bfloat16),
            pltpu.VMEM((coarse_x, coarse_ring, width), jnp.float32),
            pltpu.VMEM((coarse_x * width, coarse_ring), jnp.bfloat16),
            pltpu.VMEM((coarse_x, width, ring), jnp.float32),
            pltpu.VMEM((coarse_x, 3, big_z, ring), jnp.float32),
            pltpu.VMEM((stage, *main.shape[1:]), main.dtype),
            pltpu.VMEM((stage, *edge.shape[1:]), edge.dtype),
            pltpu.SemaphoreType.DMA((2,)),
        ],
        compiler_params=pltpu.CompilerParams(vmem_limit_bytes=60 * 1024 * 1024),
    )(main, edge, own, w1, bias, w2, pool, spread)


HALO = 16


def constants(lanes, big_z, fields):
    ring, own, coarse_z = lanes + EDGE, lanes // 2, big_z // 2
    coarse_ring = own + 2 * HALO
    covers = np.zeros((coarse_ring, ring), np.float32)
    for m in range(coarse_ring):
        first = 2 * m if m < own + HALO else ring - 2 * (coarse_ring - m)
        covers[m, first : first + 2] = 1.0
    pool = np.concatenate([covers, covers], 1) * 0.125
    block = fields * big_z
    group = max(1, 128 // block)
    slots = 3 if group == 1 else 2 * group
    first = np.zeros((big_z, coarse_z, 3), np.float32)
    second = np.zeros((coarse_z, coarse_z, 3), np.float32)
    for dz in range(3):
        for z in range(coarse_z):
            first[2 * ((z + dz - 1) % coarse_z), z, dz] = 1.0
            second[(z + dz - 1) % coarse_z, z, dz] = 1.0
    places = np.zeros((group, slots, 3), np.float32)
    for variant in range(group):
        for dx in range(3):
            places[variant, (variant - 1) % group + dx, dx] = 1.0
    return [jnp.asarray(a, jnp.bfloat16) for a in (pool, covers, first, second, places)]


def per_device(nets, wides, narrows, fields, conv1_weight, conv1_bias, conv2_weight):
    count, depth, xs, lanes = fields.shape
    big_z = depth * nets
    coarse_z = big_z // 2
    pool, spread, first, second, places = constants(lanes, big_z, count)
    own = fields.transpose(0, 2, 1, 3)
    main, edge = gather(own.astype(jnp.bfloat16).reshape(-1, lanes), nets, wides, narrows)
    hidden, channels = conv1_weight.shape[1:]
    parts = conv2_weight.shape[1]
    w1 = conv1_weight.reshape(3, 3, 3, hidden, channels)
    w1 = jnp.einsum("dxyoc,qpd,vsx->vyscqpo", w1, first, places)
    w1 = w1.reshape(places.shape[0], 3, places.shape[1] * channels * big_z, coarse_z * hidden)
    w2 = jnp.einsum("dxysh,qpd->yqhxsp", conv2_weight.reshape(3, 3, 3, parts, hidden), second)
    w2 = w2.reshape(3, coarse_z * hidden, 3, parts * coarse_z)
    width = parts * coarse_z
    width = 64 if width <= 64 else -(-width // 128) * 128
    w2 = jnp.pad(w2, ((0, 0), (0, 0), (0, 0), (0, width - parts * coarse_z))).reshape(3, coarse_z * hidden, 3 * width)
    bias = jnp.tile(conv1_bias, coarse_z)[None]
    moved = step(main, edge, own, w1, bias, w2, pool, spread, nets, wides)
    return moved.transpose(0, 2, 1, 3)


def solution(mesh):
    in_specs = (P(None, "net", "wide", "narrow"), P(), P(), P())
    out_specs = P(None, "net", "wide", "narrow")
    sizes = (mesh.shape["net"], mesh.shape["wide"], mesh.shape["narrow"])
    return jax.shard_map(
        functools.partial(per_device, *sizes), mesh=mesh, in_specs=in_specs, out_specs=out_specs, check_vma=False
    )
```

```python
import functools
import math

import jax
import jax.numpy as jnp
import numpy as np
from jax import lax
from jax.experimental import pallas as pl
from jax.experimental.pallas import tpu as pltpu
from jax.sharding import PartitionSpec as P

MESH = pl.DeviceIdType.MESH
TIME_STEP = 0.2
VISCOSITY = 0.05
EDGE = 128


def joined_weights(conv1_ref, conv2_ref, pick1_ref, pick2_ref, tile_ref, w1_ref, w2_ref, big_z):
    coarse_z = big_z // 2
    f32, bf16 = jnp.float32, jnp.bfloat16
    tile = tile_ref[...]
    hidden = tile.shape[0]
    rows, columns = w1_ref.shape[2:]
    zi = lax.broadcasted_iota(jnp.int32, (rows, columns), 0) % big_z
    zo = lax.broadcasted_iota(jnp.int32, (rows, columns), 1) // hidden
    masks1 = [zi == 2 * ((zo + dz + coarse_z - 1) % coarse_z) for dz in range(3)]
    shape2 = (w2_ref.shape[1], w2_ref.shape[2])
    width = shape2[1] // 3
    zi = lax.broadcasted_iota(jnp.int32, shape2, 0) // hidden
    zo = lax.broadcasted_iota(jnp.int32, shape2, 1) % width % coarse_z
    masks2 = [zi == (zo + dz + coarse_z - 1) % coarse_z for dz in range(3)]

    def stacked(ref, dz, dy):
        pieces = []
        for dx in range(3):
            piece = ref[9 * dz + 3 * dx + dy].astype(f32)
            pieces += [piece, jnp.zeros((8 - piece.shape[0], hidden), f32)]
        return jnp.concatenate(pieces, axis=0).astype(bf16)

    for dy in range(3):
        total = [None] * w1_ref.shape[0]
        for dz in range(3):
            spread = jnp.dot(stacked(conv1_ref, dz, dy), tile, preferred_element_type=f32).astype(bf16)
            for variant in range(len(total)):
                term = jnp.dot(pick1_ref[variant], spread, preferred_element_type=f32)
                term = jnp.where(masks1[dz], term, 0.0)
                total[variant] = term if dz == 0 else total[variant] + term
        for variant, value in enumerate(total):
            w1_ref[variant, dy] = value.astype(bf16)
        value = None
        for dz in range(3):
            repeated = jnp.dot(pick2_ref[...], stacked(conv2_ref, dz, dy), preferred_element_type=f32).astype(bf16)
            term = lax.dot_general(tile, repeated, (((0,), (1,)), ((), ())), preferred_element_type=f32)
            term = jnp.where(masks2[dz], term, 0.0)
            value = term if dz == 0 else value + term
        w2_ref[dy] = value.astype(bf16)


def gather_kernel(nets, wides, narrows, big_z, state_ref, conv1_ref, conv2_ref, pick1_ref, pick2_ref, tile_ref,
                  main_ref, edge_ref, w1_ref, w2_ref, own_ref, after, before, packed,
                  y_send, y_recv, main_send, main_recv, edge_send, edge_recv, local_sem):
    net, wide, narrow = lax.axis_index("net"), lax.axis_index("wide"), lax.axis_index("narrow")
    up, down = lax.rem(narrow + 1, narrows), lax.rem(narrow + narrows - 1, narrows)
    length = own_ref.shape[1]
    offsets = [(dn, dw) for dn in range(nets) for dw in range(wides) if (dn, dw) != (0, 0)]

    def device(n, w, k):
        return {"net": n, "wide": w, "narrow": k}

    def target(dn, dw):
        return device(lax.rem(net + nets - dn, nets), lax.rem(wide + wides - dw, wides), narrow)

    own_ref[...] = state_ref[...].astype(own_ref.dtype)
    barrier = pltpu.get_barrier_semaphore()
    for k in (up, down):
        pl.semaphore_signal(barrier, inc=1, device_id=device(net, wide, k), device_id_type=MESH)
    for dn, dw in offsets:
        pl.semaphore_signal(barrier, inc=1, device_id=target(dn, dw), device_id_type=MESH)
    pl.semaphore_wait(barrier, 2 + len(offsets))

    def remote(src, dst, send, recv, where):
        return pltpu.make_async_remote_copy(
            src_ref=src, dst_ref=dst, send_sem=send, recv_sem=recv, device_id=where, device_id_type=MESH
        )

    to_down = remote(own_ref.at[:, pl.ds(0, EDGE)], after, y_send.at[0], y_recv.at[0], device(net, wide, down))
    to_up = remote(own_ref.at[:, pl.ds(length - EDGE, EDGE)], before, y_send.at[1], y_recv.at[1], device(net, wide, up))
    to_down.start()
    to_up.start()
    mains = []
    for dn, dw in offsets:
        slot = dn * wides + dw
        mains.append(remote(own_ref, main_ref.at[slot], main_send.at[slot], main_recv.at[slot], target(dn, dw)))
        mains[-1].start()
    own_main = pltpu.make_async_copy(own_ref, main_ref.at[0], local_sem.at[0])
    own_main.start()
    to_down.wait()
    to_up.wait()
    lane = lax.broadcasted_iota(jnp.int32, after.shape, 1)
    packed[...] = jnp.where(
        lane < EDGE // 2, after[...].astype(jnp.float32), before[...].astype(jnp.float32)
    ).astype(packed.dtype)
    edges = []
    for dn, dw in offsets:
        slot = dn * wides + dw
        edges.append(remote(packed, edge_ref.at[slot], edge_send.at[slot], edge_recv.at[slot], target(dn, dw)))
        edges[-1].start()
    own_edge = pltpu.make_async_copy(packed, edge_ref.at[0], local_sem.at[1])
    own_edge.start()
    joined_weights(conv1_ref, conv2_ref, pick1_ref, pick2_ref, tile_ref, w1_ref, w2_ref, big_z)
    for copy in mains + edges + [own_main, own_edge]:
        copy.wait()


def gather(own, conv1, conv2, picks, width, big_z, nets, wides, narrows):
    rows, length = own.shape
    travel = jnp.bfloat16
    columns = picks[2].shape[1]
    slots = nets * wides
    return pl.pallas_call(
        functools.partial(gather_kernel, nets, wides, narrows, big_z),
        out_shape=[
            jax.ShapeDtypeStruct((slots, rows, length), travel),
            jax.ShapeDtypeStruct((slots, rows, EDGE), travel),
            jax.ShapeDtypeStruct((picks[0].shape[0], 3, picks[0].shape[1], columns), jnp.bfloat16),
            jax.ShapeDtypeStruct((3, columns, 3 * width), jnp.bfloat16),
        ],
        in_specs=[pl.BlockSpec(memory_space=pltpu.VMEM)] * 6,
        out_specs=[pl.BlockSpec(memory_space=pl.ANY)] * 2 + [pl.BlockSpec(memory_space=pltpu.VMEM)] * 2,
        scratch_shapes=[
            pltpu.VMEM((rows, length), travel),
            pltpu.VMEM((rows, EDGE), travel),
            pltpu.VMEM((rows, EDGE), travel),
            pltpu.VMEM((rows, EDGE), travel),
            pltpu.SemaphoreType.DMA((2,)),
            pltpu.SemaphoreType.DMA((2,)),
            pltpu.SemaphoreType.DMA((slots,)),
            pltpu.SemaphoreType.DMA((slots,)),
            pltpu.SemaphoreType.DMA((slots,)),
            pltpu.SemaphoreType.DMA((slots,)),
            pltpu.SemaphoreType.DMA((2,)),
        ],
        compiler_params=pltpu.CompilerParams(
            collective_id=0, has_side_effects=True, vmem_limit_bytes=60 * 1024 * 1024
        ),
    )(own, conv1, conv2, *picks)


def shifted(values, offset, axis):
    return pltpu.roll(values, (-offset) % values.shape[axis], axis)


def two_parts(values):
    high = values.astype(jnp.bfloat16)
    low = (values - high.astype(jnp.float32)).astype(jnp.bfloat16)
    return high, low


def gelu(x):
    inner = x * (0.7978845608028654 + 0.035677408136300125 * (x * x))
    half = 0.5 * x
    return half + half * jnp.tanh(inner)


def step_kernel(nets, wides, main_ref, edge_ref, own_ref, w1_ref, bias_ref, w2_ref, pool_ref, spread_ref,
                out_ref, base, state, thin, taps, wide_hidden, partial, turned, upper, force, mains, edges, arrived):
    fields, xs, depth, lanes = own_ref.shape
    big_x, big_z, ring = base.shape[1:]
    coarse_x, coarse_z = big_x // 2, big_z // 2
    coarse_ring = pool_ref.shape[0]
    block = fields * big_z
    part_x = thin.shape[0] // block
    stage = mains.shape[0]
    unroll = 2 if big_z <= 16 else 1
    variants, window = w1_ref.shape[0], w1_ref.shape[2]
    pad = (taps.shape[2] - coarse_x * block) // 2
    channels = w2_ref.shape[1]
    width = w2_ref.shape[2] // 3
    batch = wide_hidden.shape[0]
    together = max(1, 128 // width)
    bias = jnp.concatenate([bias_ref[...]] * coarse_z, axis=1)

    for begin in range(0, nets * wides, stage):
        copies = [
            pltpu.make_async_copy(main_ref.at[pl.ds(begin, stage)], mains, arrived.at[0]),
            pltpu.make_async_copy(edge_ref.at[pl.ds(begin, stage)], edges, arrived.at[1]),
        ]
        for copy in copies:
            copy.start()
        for copy in copies:
            copy.wait()
        for i in range(stage):
            dn, dw = divmod(begin + i, wides)
            x_at, z_at = pl.ds(dw * xs, xs), pl.ds(dn * depth, depth)
            if begin + i == 0:
                base[:, x_at, z_at, pl.ds(0, lanes)] = own_ref[...]
            else:
                base[:, x_at, z_at, pl.ds(0, lanes)] = (
                    mains[i].astype(jnp.float32).reshape(fields, xs, depth, lanes)
                )
            base[:, x_at, z_at, pl.ds(lanes, EDGE)] = (
                edges[i].astype(jnp.float32).reshape(fields, xs, depth, EDGE)
            )

    def each(count, body):
        if count == 1:
            body(0)
        else:
            pl.loop(0, count)(body)

    def wrapped(i, size):
        return (i + size) % size if isinstance(i, int) else lax.rem(i + size, size)

    def forces(src):
        @functools.partial(each, coarse_x // part_x)
        def _(turn):
            chunk = turn * part_x

            @pl.loop(0, part_x, unroll=unroll)
            def _(i):
                x = chunk + i
                for c in range(fields):
                    both = src[c, 2 * x] + src[c, 2 * x + 1]
                    both = both + shifted(both, 1, 0)
                    high, low = two_parts(both)
                    at = pl.ds(pl.multiple_of(i * block + c * big_z, big_z), big_z)
                    thin[at, pl.ds(0, ring)] = high
                    thin[at, pl.ds(ring, ring)] = low

            coarse = lax.dot_general(
                pool_ref[...], thin[...], (((1,), (1,)), ((), ())), preferred_element_type=jnp.float32
            )
            for dy in range(3):
                moved = (coarse if dy == 1 else shifted(coarse, dy - 1, 0)).astype(jnp.bfloat16)
                at = pl.multiple_of(pad + chunk * block, 128)
                taps[dy, :, pl.ds(at, part_x * block)] = moved

        span = coarse_x * block
        taps[:, :, pl.ds(0, pad)] = taps[:, :, pl.ds(span, pad)]
        taps[:, :, pl.ds(pad + span, pad)] = taps[:, :, pl.ds(pad, pad)]

        if batch < coarse_x:
            partial[...] = jnp.zeros_like(partial)

        @functools.partial(each, coarse_x // batch)
        def _(turn):
            begin = turn * batch
            for variant in range(variants):
                mine = list(range(variant, batch, variants))
                rows = []
                for x in mine:
                    at = pl.multiple_of(begin * block + (pad + (x - 1) * block) // 128 * 128, 128)
                    rows.append(jnp.concatenate([taps[dy, :, pl.ds(at, window)] for dy in range(3)], axis=1))
                around = jnp.concatenate(rows, axis=0)
                weight = w1_ref[variant].reshape(3 * window, channels)
                hidden = jnp.dot(around, weight, preferred_element_type=jnp.float32) + bias
                hidden = gelu(hidden)
                for i, x in enumerate(mine):
                    here = hidden[i * coarse_ring : (i + 1) * coarse_ring]
                    for dy in range(3):
                        moved = (here if dy == 1 else shifted(here, dy - 1, 0)).astype(jnp.bfloat16)
                        wide_hidden[x, :, pl.ds(dy * channels, channels)] = moved
            found = jnp.dot(
                wide_hidden[...].reshape(batch * coarse_ring, 3 * channels),
                w2_ref[...].reshape(3 * channels, 3 * width),
                preferred_element_type=jnp.float32,
            )
            found = found.reshape(batch, coarse_ring, 3 * width)
            for i in range(batch):
                if batch == coarse_x:
                    total = found[(i - 1) % coarse_x, :, :width] + found[i, :, width : 2 * width]
                    partial[i] = total + found[(i + 1) % coarse_x, :, 2 * width :]
                else:
                    for dx in range(3):
                        partial[wrapped(begin + i + 1 - dx, coarse_x)] += found[i, :, dx * width : (dx + 1) * width]

        def turn_over(x):
            totals = [partial[x + i] for i in range(together)]
            total = jnp.concatenate(totals, axis=1) if together > 1 else totals[0]
            at = x * width if isinstance(x, int) else pl.multiple_of(x * width, width)
            turned[pl.ds(at, together * width), :] = total.T.astype(jnp.bfloat16)

        if batch == coarse_x:
            for x in range(0, coarse_x, together):
                turn_over(x)
        else:
            pl.loop(0, coarse_x // together)(lambda i: turn_over(i * together))

        @functools.partial(each, coarse_x // batch)
        def _(turn):
            begin = turn * batch
            at = pl.multiple_of(begin * width, batch * width)
            fine = jnp.dot(
                turned[pl.ds(at, batch * width), :], spread_ref[...], preferred_element_type=jnp.float32
            )
            upper[pl.ds(begin, batch)] = fine.reshape(batch, width, ring)

        @pl.loop(0, coarse_x, unroll=unroll)
        def _(x):
            ahead, behind = wrapped(x + 1, coarse_x), wrapped(x - 1, coarse_x)

            def part(at, component):
                return upper[at, pl.ds(component * coarse_z, coarse_z)]

            for axis, (in_x, in_y, in_z) in enumerate(((0, 3, 4), (3, 1, 5), (4, 5, 2))):
                along_y, along_z = part(x, in_y), part(x, in_z)
                total = part(ahead, in_x) - part(behind, in_x)
                total = total + shifted(along_y, 2, 1) - shifted(along_y, -2, 1)
                total = 0.25 * (total + shifted(along_z, 1, 0) - shifted(along_z, -1, 0))
                force[x, axis] = jnp.broadcast_to(total[:, None], (coarse_z, 2, ring)).reshape(big_z, ring)

    def rates(src, x, give):
        ahead, behind = wrapped(x + 1, big_x), wrapped(x - 1, big_x)
        half = [0.5 * src[c, x] for c in range(3)]
        u, v, w = half
        plus = [VISCOSITY - h for h in half]
        minus = [VISCOSITY + h for h in half]
        for c in range(fields):
            q = src[c, x]
            rate = plus[0] * src[c, ahead] + minus[0] * src[c, behind]
            rate = rate + plus[1] * shifted(q, 1, 1) + minus[1] * shifted(q, -1, 1)
            rate = rate + plus[2] * shifted(q, 1, 0) + minus[2] * shifted(q, -1, 0)
            rate = rate - (6.0 * VISCOSITY) * q
            if c < 3:
                rate = rate + force[x // 2, c]
            give(c, q, rate)

    forces(base)

    @pl.loop(0, big_x, unroll=unroll)
    def _(x):
        def give(c, q, rate):
            state[c, x] = q + TIME_STEP * rate

        rates(base, x, give)

    forces(state)

    @pl.loop(0, big_x, unroll=unroll)
    def _(x):
        def give(c, q, rate):
            base[c, x] = 0.75 * base[c, x] + 0.25 * (q + TIME_STEP * rate)

        rates(state, x, give)

    forces(base)

    for x in range(xs):
        def give(c, q, rate):
            moved = (q + TIME_STEP * rate)[:depth, :lanes]
            out_ref[c, x] = own_ref[c, x] * (1.0 / 3.0) + (2.0 / 3.0) * moved

        rates(base, x, give)


def step(main, edge, own, w1, bias, w2, pool, spread, nets, wides):
    fields, xs, depth, lanes = own.shape
    big_x, big_z, ring = xs * wides, depth * nets, lanes + EDGE
    coarse_x, coarse_ring = big_x // 2, pool.shape[0]
    block = fields * big_z
    part_x = math.gcd(coarse_x, max(1, 512 // block))
    stage = math.gcd(nets * wides, 8)
    batch = math.gcd(coarse_x, 8 if block < 128 else 1)
    channels, width = w2.shape[1], w2.shape[2] // 3
    return pl.pallas_call(
        functools.partial(step_kernel, nets, wides),
        out_shape=jax.ShapeDtypeStruct(own.shape, jnp.float32),
        in_specs=[pl.BlockSpec(memory_space=pl.ANY)] * 2 + [pl.BlockSpec(memory_space=pltpu.VMEM)] * 6,
        out_specs=pl.BlockSpec(memory_space=pltpu.VMEM),
        scratch_shapes=[
            pltpu.VMEM((fields, big_x, big_z, ring), jnp.float32),
            pltpu.VMEM((fields, big_x, big_z, ring), jnp.float32),
            pltpu.VMEM((part_x * block, 2 * ring), jnp.bfloat16),
            pltpu.VMEM((3, coarse_ring, coarse_x * block + 2 * max(128, block)), jnp.bfloat16),
            pltpu.VMEM((batch, coarse_ring, 3 * channels), jnp.bfloat16),
            pltpu.VMEM((coarse_x, coarse_ring, width), jnp.float32),
            pltpu.VMEM((coarse_x * width, coarse_ring), jnp.bfloat16),
            pltpu.VMEM((coarse_x, width, ring), jnp.float32),
            pltpu.VMEM((coarse_x, 3, big_z, ring), jnp.float32),
            pltpu.VMEM((stage, *main.shape[1:]), main.dtype),
            pltpu.VMEM((stage, *edge.shape[1:]), edge.dtype),
            pltpu.SemaphoreType.DMA((2,)),
        ],
        compiler_params=pltpu.CompilerParams(vmem_limit_bytes=60 * 1024 * 1024),
    )(main, edge, own, w1, bias, w2, pool, spread)


HALO = 16


def constants(lanes, big_z, fields, hidden, parts):
    ring, own, coarse_z = lanes + EDGE, lanes // 2, big_z // 2
    coarse_ring = own + 2 * HALO
    covers = np.zeros((coarse_ring, ring), np.float32)
    for m in range(coarse_ring):
        first = 2 * m if m < own + HALO else ring - 2 * (coarse_ring - m)
        covers[m, first : first + 2] = 1.0
    pool = np.concatenate([covers, covers], 1) * 0.125
    block = fields * big_z
    group = max(1, 128 // block)
    slots = 3 if group == 1 else 2 * group
    rows = np.arange(slots * block)
    slot, channel = rows // block, rows // big_z % fields
    pick1 = np.zeros((group, slots * block, 24), np.float32)
    for variant in range(group):
        for dx in range(3):
            for c in range(fields):
                here = (slot == (variant - 1) % group + dx) & (channel == c)
                pick1[variant, here, 8 * dx + c] = 1.0
    width = parts * coarse_z
    width = 64 if width <= 64 else -(-width // 128) * 128
    pick2 = np.zeros((3 * width, 24), np.float32)
    for dx in range(3):
        for s in range(parts):
            start = dx * width + s * coarse_z
            pick2[start : start + coarse_z, 8 * dx + s] = 1.0
    tile = np.tile(np.eye(hidden, dtype=np.float32), (1, coarse_z))
    return [jnp.asarray(a, jnp.bfloat16) for a in (pool, covers, pick1, pick2, tile)]


def per_device(nets, wides, narrows, fields, conv1_weight, conv1_bias, conv2_weight):
    count, depth, xs, lanes = fields.shape
    big_z = depth * nets
    hidden, parts = conv1_weight.shape[1], conv2_weight.shape[1]
    pool, spread, *picks = constants(lanes, big_z, count, hidden, parts)
    own = fields.transpose(0, 2, 1, 3)
    main, edge, w1, w2 = gather(
        own.reshape(-1, lanes), conv1_weight.transpose(0, 2, 1), conv2_weight, picks,
        picks[1].shape[0] // 3, big_z, nets, wides, narrows,
    )
    bias = conv1_bias[None]
    moved = step(main, edge, own, w1, bias, w2, pool, spread, nets, wides)
    return moved.transpose(0, 2, 1, 3)


def solution(mesh):
    in_specs = (P(None, "net", "wide", "narrow"), P(), P(), P())
    out_specs = P(None, "net", "wide", "narrow")
    sizes = (mesh.shape["net"], mesh.shape["wide"], mesh.shape["narrow"])
    return jax.shard_map(
        functools.partial(per_device, *sizes), mesh=mesh, in_specs=in_specs, out_specs=out_specs, check_vma=False
    )
```

```python
import functools
import math

import jax
import jax.numpy as jnp
import numpy as np
from jax import lax
from jax.experimental import pallas as pl
from jax.experimental.pallas import tpu as pltpu
from jax.sharding import PartitionSpec as P

MESH = pl.DeviceIdType.MESH
TIME_STEP = 0.2
VISCOSITY = 0.05
EDGE = 128


def joined_weights(conv1_ref, conv2_ref, pick1_ref, pick2_ref, tile_ref, w1_ref, w2_ref, big_z):
    coarse_z = big_z // 2
    f32, bf16 = jnp.float32, jnp.bfloat16
    tile = tile_ref[...]
    hidden = tile.shape[0]
    rows, columns = w1_ref.shape[2:]
    zi = lax.broadcasted_iota(jnp.int32, (rows, columns), 0) % big_z
    zo = lax.broadcasted_iota(jnp.int32, (rows, columns), 1) // hidden
    masks1 = [zi == 2 * ((zo + dz + coarse_z - 1) % coarse_z) for dz in range(3)]
    shape2 = (w2_ref.shape[1], w2_ref.shape[2])
    width = shape2[1] // 3
    zi = lax.broadcasted_iota(jnp.int32, shape2, 0) // hidden
    zo = lax.broadcasted_iota(jnp.int32, shape2, 1) % width % coarse_z
    masks2 = [zi == (zo + dz + coarse_z - 1) % coarse_z for dz in range(3)]

    def stacked(ref, dz, dy):
        pieces = []
        for dx in range(3):
            piece = ref(9 * dz + 3 * dx + dy)
            pieces += [piece, jnp.zeros((8 - piece.shape[0], hidden), f32)]
        return jnp.concatenate(pieces, axis=0).astype(bf16)

    second = conv2_ref[...].astype(f32)

    def second_tap(t):
        return jnp.concatenate([second[i, t : t + 1] for i in range(second.shape[0])], axis=0)

    for dy in range(3):
        total = [None] * w1_ref.shape[0]
        for dz in range(3):
            spread = jnp.dot(stacked(lambda t: conv1_ref[t].astype(f32), dz, dy), tile, preferred_element_type=f32).astype(bf16)
            for variant in range(len(total)):
                term = jnp.dot(pick1_ref[variant], spread, preferred_element_type=f32)
                term = jnp.where(masks1[dz], term, 0.0)
                total[variant] = term if dz == 0 else total[variant] + term
        for variant, value in enumerate(total):
            w1_ref[variant, dy] = value.astype(bf16)
        value = None
        for dz in range(3):
            repeated = jnp.dot(pick2_ref[...], stacked(second_tap, dz, dy), preferred_element_type=f32).astype(bf16)
            term = lax.dot_general(tile, repeated, (((0,), (1,)), ((), ())), preferred_element_type=f32)
            term = jnp.where(masks2[dz], term, 0.0)
            value = term if dz == 0 else value + term
        w2_ref[dy] = value.astype(bf16)


def gather_kernel(nets, wides, narrows, big_z, state_ref, conv1_ref, conv2_ref, pick1_ref, pick2_ref, tile_ref,
                  main_ref, edge_ref, w1_ref, w2_ref, turned_ref, own_ref, after, before, packed,
                  y_send, y_recv, main_send, main_recv, edge_send, edge_recv, local_sem):
    net, wide, narrow = lax.axis_index("net"), lax.axis_index("wide"), lax.axis_index("narrow")
    up, down = lax.rem(narrow + 1, narrows), lax.rem(narrow + narrows - 1, narrows)
    length = own_ref.shape[1]

    def device(n, w, k):
        return {"net": n, "wide": w, "narrow": k}

    def target(dn, dw):
        return device(lax.rem(net + nets - dn, nets), lax.rem(wide + wides - dw, wides), narrow)

    core = lax.rem(wide, 2)
    partner = device(net, wide + 1 - 2 * core, narrow)
    direct = [(dn, dw) for dn in range(nets) for dw in range(0, wides, 2) if (dn, dw) != (0, 0)]
    handed = [dn * wides + dw for dn in range(nets) for dw in range(1, wides, 2)]

    barrier = pltpu.get_barrier_semaphore()
    for k in (up, down):
        pl.semaphore_signal(barrier, inc=1, device_id=device(net, wide, k), device_id_type=MESH)
    for dn, dw in direct:
        pl.semaphore_signal(barrier, inc=1, device_id=target(dn, dw), device_id_type=MESH)
    pl.semaphore_signal(barrier, inc=1, device_id=partner, device_id_type=MESH)
    for f in range(state_ref.shape[0]):
        for x in range(state_ref.shape[2]):
            turned_ref[f, x] = state_ref[f, :, x, :]
    own_ref[...] = turned_ref[...].reshape(own_ref.shape).astype(own_ref.dtype)
    pl.semaphore_wait(barrier, 3 + len(direct))

    def remote(src, dst, send, recv, where):
        return pltpu.make_async_remote_copy(
            src_ref=src, dst_ref=dst, send_sem=send, recv_sem=recv, device_id=where, device_id_type=MESH
        )

    to_down = remote(own_ref.at[:, pl.ds(0, EDGE)], after, y_send.at[0], y_recv.at[0], device(net, wide, down))
    to_up = remote(own_ref.at[:, pl.ds(length - EDGE, EDGE)], before, y_send.at[1], y_recv.at[1], device(net, wide, up))
    to_down.start()
    to_up.start()
    def hand_on(src, ref, dn, dw, send, recv):
        slot = dn * wides + lax.rem(dw + wides - 1 + 2 * core, wides)
        return remote(src, ref.at[slot], send.at[slot], recv.at[slot], partner)

    mains, sent = [], []
    for dn, dw in direct:
        slot = dn * wides + dw
        mains.append(remote(own_ref, main_ref.at[slot], main_send.at[slot], main_recv.at[slot], target(dn, dw)))
        mains[-1].start()
    sent.append(hand_on(own_ref, main_ref, 0, 0, main_send, main_recv))
    sent[-1].start()
    own_main = pltpu.make_async_copy(own_ref, main_ref.at[0], local_sem.at[0])
    own_main.start()
    to_down.wait()
    to_up.wait()
    lane = lax.broadcasted_iota(jnp.int32, after.shape, 1)
    packed[...] = jnp.where(
        lane < EDGE // 2, after[...].astype(jnp.float32), before[...].astype(jnp.float32)
    ).astype(packed.dtype)
    edges = []
    for dn, dw in direct:
        slot = dn * wides + dw
        edges.append(remote(packed, edge_ref.at[slot], edge_send.at[slot], edge_recv.at[slot], target(dn, dw)))
        edges[-1].start()
    sent.append(hand_on(packed, edge_ref, 0, 0, edge_send, edge_recv))
    sent[-1].start()
    own_edge = pltpu.make_async_copy(packed, edge_ref.at[0], local_sem.at[1])
    own_edge.start()
    joined_weights(conv1_ref, conv2_ref, pick1_ref, pick2_ref, tile_ref, w1_ref, w2_ref, big_z)
    for copies, ref, send, recv in ((mains, main_ref, main_send, main_recv), (edges, edge_ref, edge_send, edge_recv)):
        for copy, (dn, dw) in zip(copies, direct):
            copy.wait_recv()
            sent.append(hand_on(ref.at[dn * wides + dw], ref, dn, dw, send, recv))
            sent[-1].start()
    for copy in mains + edges + sent:
        copy.wait_send()
    for slot in handed:
        remote(main_ref.at[slot], main_ref.at[slot], main_send.at[slot], main_recv.at[slot], partner).wait_recv()
        remote(edge_ref.at[slot], edge_ref.at[slot], edge_send.at[slot], edge_recv.at[slot], partner).wait_recv()
    own_main.wait()
    own_edge.wait()


def gather(own, conv1, conv2, picks, width, big_z, nets, wides, narrows):
    count, depth, xs, length = own.shape
    rows = count * depth * xs
    travel = jnp.bfloat16
    columns = picks[2].shape[1]
    slots = nets * wides
    return pl.pallas_call(
        functools.partial(gather_kernel, nets, wides, narrows, big_z),
        out_shape=[
            jax.ShapeDtypeStruct((slots, rows, length), travel),
            jax.ShapeDtypeStruct((slots, rows, EDGE), travel),
            jax.ShapeDtypeStruct((picks[0].shape[0], 3, picks[0].shape[1], columns), jnp.bfloat16),
            jax.ShapeDtypeStruct((3, columns, 3 * width), jnp.bfloat16),
            jax.ShapeDtypeStruct((count, xs, depth, length), jnp.float32),
        ],
        in_specs=[pl.BlockSpec(memory_space=pltpu.VMEM)] * 6,
        out_specs=[pl.BlockSpec(memory_space=pl.ANY)] * 2 + [pl.BlockSpec(memory_space=pltpu.VMEM)] * 3,
        scratch_shapes=[
            pltpu.VMEM((rows, length), travel),
            pltpu.VMEM((rows, EDGE), travel),
            pltpu.VMEM((rows, EDGE), travel),
            pltpu.VMEM((rows, EDGE), travel),
            pltpu.SemaphoreType.DMA((2,)),
            pltpu.SemaphoreType.DMA((2,)),
            pltpu.SemaphoreType.DMA((slots,)),
            pltpu.SemaphoreType.DMA((slots,)),
            pltpu.SemaphoreType.DMA((slots,)),
            pltpu.SemaphoreType.DMA((slots,)),
            pltpu.SemaphoreType.DMA((2,)),
        ],
        compiler_params=pltpu.CompilerParams(
            collective_id=0, has_side_effects=True, vmem_limit_bytes=60 * 1024 * 1024
        ),
    )(own, conv1, conv2, *picks)


def shifted(values, offset, axis):
    return pltpu.roll(values, (-offset) % values.shape[axis], axis)


def two_parts(values):
    high = values.astype(jnp.bfloat16)
    low = (values - high.astype(jnp.float32)).astype(jnp.bfloat16)
    return high, low


def gelu(x):
    inner = x * (0.7978845608028654 + 0.035677408136300125 * (x * x))
    half = 0.5 * x
    return half + half * jnp.tanh(inner)


def step_kernel(nets, wides, main_ref, edge_ref, own_ref, w1_ref, bias_ref, w2_ref, pool_ref, spread_ref,
                out_ref, base, state, thin, taps, wide_hidden, partial, turned, upper, force, mains, edges, arrived):
    fields, xs, depth, lanes = own_ref.shape
    big_x, big_z, ring = base.shape[1:]
    coarse_x, coarse_z = big_x // 2, big_z // 2
    coarse_ring = pool_ref.shape[0]
    block = fields * big_z
    part_x = thin.shape[0] // block
    stage = mains.shape[0]
    unroll = 2 if big_z <= 16 else 1
    variants, window = w1_ref.shape[0], w1_ref.shape[2]
    pad = (taps.shape[2] - coarse_x * block) // 2
    channels = w2_ref.shape[1]
    width = w2_ref.shape[2] // 3
    batch = wide_hidden.shape[0]
    together = max(1, 128 // width)
    bias = jnp.concatenate([bias_ref[...]] * coarse_z, axis=1)

    for begin in range(0, nets * wides, stage):
        copies = [
            pltpu.make_async_copy(main_ref.at[pl.ds(begin, stage)], mains, arrived.at[0]),
            pltpu.make_async_copy(edge_ref.at[pl.ds(begin, stage)], edges, arrived.at[1]),
        ]
        for copy in copies:
            copy.start()
        for copy in copies:
            copy.wait()
        for i in range(stage):
            dn, dw = divmod(begin + i, wides)
            x_at, z_at = pl.ds(dw * xs, xs), pl.ds(dn * depth, depth)
            if begin + i == 0:
                base[:, x_at, z_at, pl.ds(0, lanes)] = own_ref[...]
            else:
                base[:, x_at, z_at, pl.ds(0, lanes)] = (
                    mains[i].astype(jnp.float32).reshape(fields, xs, depth, lanes)
                )
            base[:, x_at, z_at, pl.ds(lanes, EDGE)] = (
                edges[i].astype(jnp.float32).reshape(fields, xs, depth, EDGE)
            )

    def each(count, body):
        if count == 1:
            body(0)
        else:
            pl.loop(0, count)(body)

    def wrapped(i, size):
        return (i + size) % size if isinstance(i, int) else lax.rem(i + size, size)

    def forces(src):
        @functools.partial(each, coarse_x // part_x)
        def _(turn):
            chunk = turn * part_x

            @pl.loop(0, part_x, unroll=unroll)
            def _(i):
                x = chunk + i
                for c in range(fields):
                    both = src[c, 2 * x] + src[c, 2 * x + 1]
                    both = both + shifted(both, 1, 0)
                    high, low = two_parts(both)
                    at = pl.ds(pl.multiple_of(i * block + c * big_z, big_z), big_z)
                    thin[at, pl.ds(0, ring)] = high
                    thin[at, pl.ds(ring, ring)] = low

            coarse = lax.dot_general(
                pool_ref[...], thin[...], (((1,), (1,)), ((), ())), preferred_element_type=jnp.float32
            )
            for dy in range(3):
                moved = (coarse if dy == 1 else shifted(coarse, dy - 1, 0)).astype(jnp.bfloat16)
                at = pl.multiple_of(pad + chunk * block, 128)
                taps[dy, :, pl.ds(at, part_x * block)] = moved

        span = coarse_x * block
        taps[:, :, pl.ds(0, pad)] = taps[:, :, pl.ds(span, pad)]
        taps[:, :, pl.ds(pad + span, pad)] = taps[:, :, pl.ds(pad, pad)]

        if batch < coarse_x:
            partial[...] = jnp.zeros_like(partial)

        @functools.partial(each, coarse_x // batch)
        def _(turn):
            begin = turn * batch
            for variant in range(variants):
                mine = list(range(variant, batch, variants))
                rows = []
                for x in mine:
                    at = pl.multiple_of(begin * block + (pad + (x - 1) * block) // 128 * 128, 128)
                    rows.append(jnp.concatenate([taps[dy, :, pl.ds(at, window)] for dy in range(3)], axis=1))
                around = jnp.concatenate(rows, axis=0)
                weight = w1_ref[variant].reshape(3 * window, channels)
                hidden = jnp.dot(around, weight, preferred_element_type=jnp.float32) + bias
                hidden = gelu(hidden)
                for i, x in enumerate(mine):
                    here = hidden[i * coarse_ring : (i + 1) * coarse_ring]
                    for dy in range(3):
                        moved = (here if dy == 1 else shifted(here, dy - 1, 0)).astype(jnp.bfloat16)
                        wide_hidden[x, :, pl.ds(dy * channels, channels)] = moved
            found = jnp.dot(
                wide_hidden[...].reshape(batch * coarse_ring, 3 * channels),
                w2_ref[...].reshape(3 * channels, 3 * width),
                preferred_element_type=jnp.float32,
            )
            found = found.reshape(batch, coarse_ring, 3 * width)
            for i in range(batch):
                if batch == coarse_x:
                    total = found[(i - 1) % coarse_x, :, :width] + found[i, :, width : 2 * width]
                    partial[i] = total + found[(i + 1) % coarse_x, :, 2 * width :]
                else:
                    for dx in range(3):
                        partial[wrapped(begin + i + 1 - dx, coarse_x)] += found[i, :, dx * width : (dx + 1) * width]

        def turn_over(x):
            totals = [partial[x + i] for i in range(together)]
            total = jnp.concatenate(totals, axis=1) if together > 1 else totals[0]
            at = x * width if isinstance(x, int) else pl.multiple_of(x * width, width)
            turned[pl.ds(at, together * width), :] = total.T.astype(jnp.bfloat16)

        if batch == coarse_x:
            for x in range(0, coarse_x, together):
                turn_over(x)
        else:
            pl.loop(0, coarse_x // together)(lambda i: turn_over(i * together))

        @functools.partial(each, coarse_x // batch)
        def _(turn):
            begin = turn * batch
            at = pl.multiple_of(begin * width, batch * width)
            fine = jnp.dot(
                turned[pl.ds(at, batch * width), :], spread_ref[...], preferred_element_type=jnp.float32
            )
            upper[pl.ds(begin, batch)] = fine.reshape(batch, width, ring)

        @pl.loop(0, coarse_x, unroll=unroll)
        def _(x):
            ahead, behind = wrapped(x + 1, coarse_x), wrapped(x - 1, coarse_x)

            def part(at, component):
                return upper[at, pl.ds(component * coarse_z, coarse_z)]

            for axis, (in_x, in_y, in_z) in enumerate(((0, 3, 4), (3, 1, 5), (4, 5, 2))):
                along_y, along_z = part(x, in_y), part(x, in_z)
                total = part(ahead, in_x) - part(behind, in_x)
                total = total + shifted(along_y, 2, 1) - shifted(along_y, -2, 1)
                total = 0.25 * (total + shifted(along_z, 1, 0) - shifted(along_z, -1, 0))
                force[x, axis] = jnp.broadcast_to(total[:, None], (coarse_z, 2, ring)).reshape(big_z, ring)

    def rates(src, x, give):
        ahead, behind = wrapped(x + 1, big_x), wrapped(x - 1, big_x)
        half = [0.5 * src[c, x] for c in range(3)]
        u, v, w = half
        plus = [VISCOSITY - h for h in half]
        minus = [VISCOSITY + h for h in half]
        for c in range(fields):
            q = src[c, x]
            rate = plus[0] * src[c, ahead] + minus[0] * src[c, behind]
            rate = rate + plus[1] * shifted(q, 1, 1) + minus[1] * shifted(q, -1, 1)
            rate = rate + plus[2] * shifted(q, 1, 0) + minus[2] * shifted(q, -1, 0)
            rate = rate - (6.0 * VISCOSITY) * q
            if c < 3:
                rate = rate + force[x // 2, c]
            give(c, q, rate)

    forces(base)

    @pl.loop(0, big_x, unroll=unroll)
    def _(x):
        def give(c, q, rate):
            state[c, x] = q + TIME_STEP * rate

        rates(base, x, give)

    forces(state)

    @pl.loop(0, big_x, unroll=unroll)
    def _(x):
        def give(c, q, rate):
            base[c, x] = 0.75 * base[c, x] + 0.25 * (q + TIME_STEP * rate)

        rates(state, x, give)

    forces(base)

    for x in range(xs):
        def give(c, q, rate):
            moved = (q + TIME_STEP * rate)[:depth, :lanes]
            out_ref[c, :, x, :] = own_ref[c, x] * (1.0 / 3.0) + (2.0 / 3.0) * moved

        rates(base, x, give)


def step(main, edge, own, w1, bias, w2, pool, spread, nets, wides):
    fields, xs, depth, lanes = own.shape
    big_x, big_z, ring = xs * wides, depth * nets, lanes + EDGE
    coarse_x, coarse_ring = big_x // 2, pool.shape[0]
    block = fields * big_z
    part_x = math.gcd(coarse_x, max(1, 512 // block))
    stage = math.gcd(nets * wides, 8)
    batch = math.gcd(coarse_x, 8 if block < 128 else 1)
    channels, width = w2.shape[1], w2.shape[2] // 3
    return pl.pallas_call(
        functools.partial(step_kernel, nets, wides),
        out_shape=jax.ShapeDtypeStruct((fields, depth, xs, lanes), jnp.float32),
        in_specs=[pl.BlockSpec(memory_space=pl.ANY)] * 2 + [pl.BlockSpec(memory_space=pltpu.VMEM)] * 6,
        out_specs=pl.BlockSpec(memory_space=pltpu.VMEM),
        scratch_shapes=[
            pltpu.VMEM((fields, big_x, big_z, ring), jnp.float32),
            pltpu.VMEM((fields, big_x, big_z, ring), jnp.float32),
            pltpu.VMEM((part_x * block, 2 * ring), jnp.bfloat16),
            pltpu.VMEM((3, coarse_ring, coarse_x * block + 2 * max(128, block)), jnp.bfloat16),
            pltpu.VMEM((batch, coarse_ring, 3 * channels), jnp.bfloat16),
            pltpu.VMEM((coarse_x, coarse_ring, width), jnp.float32),
            pltpu.VMEM((coarse_x * width, coarse_ring), jnp.bfloat16),
            pltpu.VMEM((coarse_x, width, ring), jnp.float32),
            pltpu.VMEM((coarse_x, 3, big_z, ring), jnp.float32),
            pltpu.VMEM((stage, *main.shape[1:]), main.dtype),
            pltpu.VMEM((stage, *edge.shape[1:]), edge.dtype),
            pltpu.SemaphoreType.DMA((2,)),
        ],
        compiler_params=pltpu.CompilerParams(vmem_limit_bytes=60 * 1024 * 1024),
    )(main, edge, own, w1, bias, w2, pool, spread)


HALO = 16


def constants(lanes, big_z, fields, hidden, parts):
    ring, own, coarse_z = lanes + EDGE, lanes // 2, big_z // 2
    coarse_ring = own + 2 * HALO
    covers = np.zeros((coarse_ring, ring), np.float32)
    for m in range(coarse_ring):
        first = 2 * m if m < own + HALO else ring - 2 * (coarse_ring - m)
        covers[m, first : first + 2] = 1.0
    pool = np.concatenate([covers, covers], 1) * 0.125
    block = fields * big_z
    group = max(1, 128 // block)
    slots = 3 if group == 1 else 2 * group
    rows = np.arange(slots * block)
    slot, channel = rows // block, rows // big_z % fields
    pick1 = np.zeros((group, slots * block, 24), np.float32)
    for variant in range(group):
        for dx in range(3):
            for c in range(fields):
                here = (slot == (variant - 1) % group + dx) & (channel == c)
                pick1[variant, here, 8 * dx + c] = 1.0
    width = parts * coarse_z
    width = 64 if width <= 64 else -(-width // 128) * 128
    pick2 = np.zeros((3 * width, 24), np.float32)
    for dx in range(3):
        for s in range(parts):
            start = dx * width + s * coarse_z
            pick2[start : start + coarse_z, 8 * dx + s] = 1.0
    tile = np.tile(np.eye(hidden, dtype=np.float32), (1, coarse_z))
    return [jnp.asarray(a, jnp.bfloat16) for a in (pool, covers, pick1, pick2, tile)]


def per_device(nets, wides, narrows, fields, conv1_weight, conv1_bias, conv2_weight):
    count, depth, xs, lanes = fields.shape
    big_z = depth * nets
    hidden, parts = conv1_weight.shape[1], conv2_weight.shape[1]
    pool, spread, *picks = constants(lanes, big_z, count, hidden, parts)
    main, edge, w1, w2, own = gather(
        fields, conv1_weight.transpose(0, 2, 1), conv2_weight.transpose(1, 0, 2), picks,
        picks[1].shape[0] // 3, big_z, nets, wides, narrows,
    )
    bias = conv1_bias[None]
    return step(main, edge, own, w1, bias, w2, pool, spread, nets, wides)


def solution(mesh):
    in_specs = (P(None, "net", "wide", "narrow"), P(), P(), P())
    out_specs = P(None, "net", "wide", "narrow")
    sizes = (mesh.shape["net"], mesh.shape["wide"], mesh.shape["narrow"])
    return jax.shard_map(
        functools.partial(per_device, *sizes), mesh=mesh, in_specs=in_specs, out_specs=out_specs, check_vma=False
    )
```

```python
import functools
import math

import jax
import jax.numpy as jnp
import numpy as np
from jax import lax
from jax.experimental import pallas as pl
from jax.experimental.pallas import tpu as pltpu
from jax.sharding import PartitionSpec as P

MESH = pl.DeviceIdType.MESH
TIME_STEP = 0.2
VISCOSITY = 0.05
EDGE = 128


def joined_weights(conv1_ref, conv2_ref, pick1_ref, pick2_ref, tile_ref, w1_ref, w2_ref, big_z):
    coarse_z = big_z // 2
    f32, bf16 = jnp.float32, jnp.bfloat16
    tile = tile_ref[...]
    hidden = tile.shape[0]
    rows, columns = w1_ref.shape[2:]
    zi = lax.broadcasted_iota(jnp.int32, (rows, columns), 0) % big_z
    zo = lax.broadcasted_iota(jnp.int32, (rows, columns), 1) // hidden
    masks1 = [zi == 2 * ((zo + dz + coarse_z - 1) % coarse_z) for dz in range(3)]
    shape2 = (w2_ref.shape[1], w2_ref.shape[2])
    width = shape2[1] // 3
    zi = lax.broadcasted_iota(jnp.int32, shape2, 0) // hidden
    zo = lax.broadcasted_iota(jnp.int32, shape2, 1) % width % coarse_z
    masks2 = [zi == (zo + dz + coarse_z - 1) % coarse_z for dz in range(3)]

    def stacked(ref, dz, dy):
        pieces = []
        for dx in range(3):
            piece = ref(9 * dz + 3 * dx + dy)
            pieces += [piece, jnp.zeros((8 - piece.shape[0], hidden), f32)]
        return jnp.concatenate(pieces, axis=0).astype(bf16)

    second = conv2_ref[...].astype(f32)

    def second_tap(t):
        return jnp.concatenate([second[i, t : t + 1] for i in range(second.shape[0])], axis=0)

    def build(dy):
        total = [None] * w1_ref.shape[0]
        for dz in range(3):
            spread = jnp.dot(stacked(lambda t: conv1_ref[t].astype(f32), dz, dy), tile, preferred_element_type=f32).astype(bf16)
            for variant in range(len(total)):
                term = jnp.dot(pick1_ref[variant], spread, preferred_element_type=f32)
                term = jnp.where(masks1[dz], term, 0.0)
                total[variant] = term if dz == 0 else total[variant] + term
        for variant, value in enumerate(total):
            w1_ref[variant, dy] = value.astype(bf16)
        value = None
        for dz in range(3):
            repeated = jnp.dot(pick2_ref[...], stacked(second_tap, dz, dy), preferred_element_type=f32).astype(bf16)
            term = lax.dot_general(tile, repeated, (((0,), (1,)), ((), ())), preferred_element_type=f32)
            term = jnp.where(masks2[dz], term, 0.0)
            value = term if dz == 0 else value + term
        w2_ref[dy] = value.astype(bf16)

    return build


def gather_kernel(nets, wides, narrows, big_z, state_ref, conv1_ref, conv2_ref, pick1_ref, pick2_ref, tile_ref,
                  main_ref, edge_ref, w1_ref, w2_ref, turned_ref, own_ref, after, before, packed,
                  y_send, y_recv, main_send, main_recv, edge_send, edge_recv, local_sem):
    net, wide, narrow = lax.axis_index("net"), lax.axis_index("wide"), lax.axis_index("narrow")
    up, down = lax.rem(narrow + 1, narrows), lax.rem(narrow + narrows - 1, narrows)
    length = own_ref.shape[1]

    def device(n, w, k):
        return {"net": n, "wide": w, "narrow": k}

    def target(dn, dw):
        return device(lax.rem(net + nets - dn, nets), lax.rem(wide + wides - dw, wides), narrow)

    core = lax.rem(wide, 2)
    partner = device(net, wide + 1 - 2 * core, narrow)
    direct = [(dn, dw) for dn in range(nets) for dw in range(0, wides, 2) if (dn, dw) != (0, 0)]
    handed = [dn * wides + dw for dn in range(nets) for dw in range(1, wides, 2)]

    barrier = pltpu.get_barrier_semaphore()
    for k in (up, down):
        pl.semaphore_signal(barrier, inc=1, device_id=device(net, wide, k), device_id_type=MESH)
    for dn, dw in direct:
        pl.semaphore_signal(barrier, inc=1, device_id=target(dn, dw), device_id_type=MESH)
    pl.semaphore_signal(barrier, inc=1, device_id=partner, device_id_type=MESH)
    for f in range(state_ref.shape[0]):
        for x in range(state_ref.shape[2]):
            turned_ref[f, x] = state_ref[f, :, x, :]
    own_ref[...] = turned_ref[...].reshape(own_ref.shape).astype(own_ref.dtype)
    pl.semaphore_wait(barrier, 3 + len(direct))

    def remote(src, dst, send, recv, where):
        return pltpu.make_async_remote_copy(
            src_ref=src, dst_ref=dst, send_sem=send, recv_sem=recv, device_id=where, device_id_type=MESH
        )

    to_down = remote(own_ref.at[:, pl.ds(0, EDGE)], after, y_send.at[0], y_recv.at[0], device(net, wide, down))
    to_up = remote(own_ref.at[:, pl.ds(length - EDGE, EDGE)], before, y_send.at[1], y_recv.at[1], device(net, wide, up))
    to_down.start()
    to_up.start()
    def hand_on(src, ref, dn, dw, send, recv):
        slot = dn * wides + lax.rem(dw + wides - 1 + 2 * core, wides)
        return remote(src, ref.at[slot], send.at[slot], recv.at[slot], partner)

    mains, sent = [], []
    for dn, dw in direct:
        slot = dn * wides + dw
        mains.append(remote(own_ref, main_ref.at[slot], main_send.at[slot], main_recv.at[slot], target(dn, dw)))
        mains[-1].start()
    sent.append(hand_on(own_ref, main_ref, 0, 0, main_send, main_recv))
    sent[-1].start()
    own_main = pltpu.make_async_copy(own_ref, main_ref.at[0], local_sem.at[0])
    own_main.start()
    build = joined_weights(conv1_ref, conv2_ref, pick1_ref, pick2_ref, tile_ref, w1_ref, w2_ref, big_z)
    build(0)
    to_down.wait()
    to_up.wait()
    lane = lax.broadcasted_iota(jnp.int32, after.shape, 1)
    packed[...] = jnp.where(
        lane < EDGE // 2, after[...].astype(jnp.float32), before[...].astype(jnp.float32)
    ).astype(packed.dtype)
    edges = []
    for dn, dw in direct:
        slot = dn * wides + dw
        edges.append(remote(packed, edge_ref.at[slot], edge_send.at[slot], edge_recv.at[slot], target(dn, dw)))
        edges[-1].start()
    sent.append(hand_on(packed, edge_ref, 0, 0, edge_send, edge_recv))
    sent[-1].start()
    own_edge = pltpu.make_async_copy(packed, edge_ref.at[0], local_sem.at[1])
    own_edge.start()
    build(1)
    for copies, ref, send, recv in ((mains, main_ref, main_send, main_recv), (edges, edge_ref, edge_send, edge_recv)):
        for copy, (dn, dw) in zip(copies, direct):
            copy.wait_recv()
            sent.append(hand_on(ref.at[dn * wides + dw], ref, dn, dw, send, recv))
            sent[-1].start()
        if ref is main_ref:
            build(2)
    for copy in mains + edges + sent:
        copy.wait_send()
    for slot in handed:
        remote(main_ref.at[slot], main_ref.at[slot], main_send.at[slot], main_recv.at[slot], partner).wait_recv()
        remote(edge_ref.at[slot], edge_ref.at[slot], edge_send.at[slot], edge_recv.at[slot], partner).wait_recv()
    own_main.wait()
    own_edge.wait()


def gather(own, conv1, conv2, picks, width, big_z, nets, wides, narrows):
    count, depth, xs, length = own.shape
    rows = count * depth * xs
    travel = jnp.bfloat16
    columns = picks[2].shape[1]
    slots = nets * wides
    return pl.pallas_call(
        functools.partial(gather_kernel, nets, wides, narrows, big_z),
        out_shape=[
            jax.ShapeDtypeStruct((slots, rows, length), travel),
            jax.ShapeDtypeStruct((slots, rows, EDGE), travel),
            jax.ShapeDtypeStruct((picks[0].shape[0], 3, picks[0].shape[1], columns), jnp.bfloat16),
            jax.ShapeDtypeStruct((3, columns, 3 * width), jnp.bfloat16),
            jax.ShapeDtypeStruct((count, xs, depth, length), jnp.float32),
        ],
        in_specs=[pl.BlockSpec(memory_space=pltpu.VMEM)] * 6,
        out_specs=[pl.BlockSpec(memory_space=pl.ANY)] * 2 + [pl.BlockSpec(memory_space=pltpu.VMEM)] * 3,
        scratch_shapes=[
            pltpu.VMEM((rows, length), travel),
            pltpu.VMEM((rows, EDGE), travel),
            pltpu.VMEM((rows, EDGE), travel),
            pltpu.VMEM((rows, EDGE), travel),
            pltpu.SemaphoreType.DMA((2,)),
            pltpu.SemaphoreType.DMA((2,)),
            pltpu.SemaphoreType.DMA((slots,)),
            pltpu.SemaphoreType.DMA((slots,)),
            pltpu.SemaphoreType.DMA((slots,)),
            pltpu.SemaphoreType.DMA((slots,)),
            pltpu.SemaphoreType.DMA((2,)),
        ],
        compiler_params=pltpu.CompilerParams(
            collective_id=0, has_side_effects=True, vmem_limit_bytes=60 * 1024 * 1024
        ),
    )(own, conv1, conv2, *picks)


def shifted(values, offset, axis):
    return pltpu.roll(values, (-offset) % values.shape[axis], axis)


def two_parts(values):
    high = values.astype(jnp.bfloat16)
    low = (values - high.astype(jnp.float32)).astype(jnp.bfloat16)
    return high, low


def gelu(x):
    inner = x * (0.7978845608028654 + 0.035677408136300125 * (x * x))
    half = 0.5 * x
    return half + half * jnp.tanh(inner)


def step_kernel(nets, wides, main_ref, edge_ref, own_ref, w1_ref, bias_ref, w2_ref, pool_ref, spread_ref,
                out_ref, base, state, thin, taps, wide_hidden, partial, turned, upper, force, mains, edges, arrived):
    fields, xs, depth, lanes = own_ref.shape
    big_x, big_z, ring = base.shape[1:]
    coarse_x, coarse_z = big_x // 2, big_z // 2
    coarse_ring = pool_ref.shape[0]
    block = fields * big_z
    part_x = thin.shape[0] // block
    stage = mains.shape[0]
    unroll = 2 if big_z <= 16 else 1
    variants, window = w1_ref.shape[0], w1_ref.shape[2]
    pad = (taps.shape[2] - coarse_x * block) // 2
    channels = w2_ref.shape[1]
    width = w2_ref.shape[2] // 3
    batch = wide_hidden.shape[0]
    together = max(1, 128 // width)
    bias = jnp.concatenate([bias_ref[...]] * coarse_z, axis=1)

    for begin in range(0, nets * wides, stage):
        copies = [
            pltpu.make_async_copy(main_ref.at[pl.ds(begin, stage)], mains, arrived.at[0]),
            pltpu.make_async_copy(edge_ref.at[pl.ds(begin, stage)], edges, arrived.at[1]),
        ]
        for copy in copies:
            copy.start()
        for copy in copies:
            copy.wait()
        for i in range(stage):
            dn, dw = divmod(begin + i, wides)
            x_at, z_at = pl.ds(dw * xs, xs), pl.ds(dn * depth, depth)
            if begin + i == 0:
                base[:, x_at, z_at, pl.ds(0, lanes)] = own_ref[...]
            else:
                base[:, x_at, z_at, pl.ds(0, lanes)] = (
                    mains[i].astype(jnp.float32).reshape(fields, xs, depth, lanes)
                )
            base[:, x_at, z_at, pl.ds(lanes, EDGE)] = (
                edges[i].astype(jnp.float32).reshape(fields, xs, depth, EDGE)
            )

    def each(count, body):
        if count == 1:
            body(0)
        else:
            pl.loop(0, count)(body)

    def wrapped(i, size):
        return (i + size) % size if isinstance(i, int) else lax.rem(i + size, size)

    def forces(src, last=False):
        own_x = xs // 2
        whole = batch < coarse_x or not last
        inner = [x for x in range(coarse_x) if whole or (x + 2) % coarse_x < own_x + 4]
        outer = [x for x in range(coarse_x) if whole or (x + 1) % coarse_x < own_x + 2]

        @functools.partial(each, coarse_x // part_x)
        def _(turn):
            chunk = turn * part_x

            @pl.loop(0, part_x, unroll=unroll)
            def _(i):
                x = chunk + i
                for c in range(fields):
                    both = src[c, 2 * x] + src[c, 2 * x + 1]
                    both = both + shifted(both, 1, 0)
                    high, low = two_parts(both)
                    at = pl.ds(pl.multiple_of(i * block + c * big_z, big_z), big_z)
                    thin[at, pl.ds(0, ring)] = high
                    thin[at, pl.ds(ring, ring)] = low

            coarse = lax.dot_general(
                pool_ref[...], thin[...], (((1,), (1,)), ((), ())), preferred_element_type=jnp.float32
            )
            for dy in range(3):
                moved = (coarse if dy == 1 else shifted(coarse, dy - 1, 0)).astype(jnp.bfloat16)
                at = pl.multiple_of(pad + chunk * block, 128)
                taps[dy, :, pl.ds(at, part_x * block)] = moved

        span = coarse_x * block
        taps[:, :, pl.ds(0, pad)] = taps[:, :, pl.ds(span, pad)]
        taps[:, :, pl.ds(pad + span, pad)] = taps[:, :, pl.ds(pad, pad)]

        if batch < coarse_x:
            partial[...] = jnp.zeros_like(partial)

        @functools.partial(each, coarse_x // batch)
        def _(turn):
            begin = turn * batch
            for variant in range(variants):
                mine = [x for x in range(variant, batch, variants) if batch < coarse_x or x in inner]
                rows = []
                for x in mine:
                    at = pl.multiple_of(begin * block + (pad + (x - 1) * block) // 128 * 128, 128)
                    rows.append(jnp.concatenate([taps[dy, :, pl.ds(at, window)] for dy in range(3)], axis=1))
                around = jnp.concatenate(rows, axis=0)
                weight = w1_ref[variant].reshape(3 * window, channels)
                hidden = jnp.dot(around, weight, preferred_element_type=jnp.float32) + bias
                hidden = gelu(hidden)
                for i, x in enumerate(mine):
                    here = hidden[i * coarse_ring : (i + 1) * coarse_ring]
                    for dy in range(3):
                        moved = (here if dy == 1 else shifted(here, dy - 1, 0)).astype(jnp.bfloat16)
                        wide_hidden[x, :, pl.ds(dy * channels, channels)] = moved
            used = range(batch) if batch < coarse_x else inner
            found = jnp.dot(
                jnp.concatenate([wide_hidden[x] for x in used], axis=0),
                w2_ref[...].reshape(3 * channels, 3 * width),
                preferred_element_type=jnp.float32,
            )
            found = found.reshape(len(used), coarse_ring, 3 * width)
            for i in range(batch):
                if batch == coarse_x:
                    if i in outer:
                        left, here, right = [inner.index((i + d) % coarse_x) for d in (-1, 0, 1)]
                        total = found[left, :, :width] + found[here, :, width : 2 * width]
                        partial[i] = total + found[right, :, 2 * width :]
                else:
                    for dx in range(3):
                        partial[wrapped(begin + i + 1 - dx, coarse_x)] += found[i, :, dx * width : (dx + 1) * width]

        def turn_over(x):
            totals = [partial[x + i] for i in range(together)]
            total = jnp.concatenate(totals, axis=1) if together > 1 else totals[0]
            at = x * width if isinstance(x, int) else pl.multiple_of(x * width, width)
            turned[pl.ds(at, together * width), :] = total.T.astype(jnp.bfloat16)

        if batch == coarse_x:
            for x in range(0, coarse_x, together):
                if any(x + i in outer for i in range(together)):
                    turn_over(x)
        else:
            pl.loop(0, coarse_x // together)(lambda i: turn_over(i * together))

        @functools.partial(each, coarse_x // batch)
        def _(turn):
            begin = turn * batch
            at = pl.multiple_of(begin * width, batch * width)
            fine = jnp.dot(
                turned[pl.ds(at, batch * width), :], spread_ref[...], preferred_element_type=jnp.float32
            )
            upper[pl.ds(begin, batch)] = fine.reshape(batch, width, ring)

        @pl.loop(0, own_x if last else coarse_x, unroll=unroll)
        def _(x):
            ahead, behind = wrapped(x + 1, coarse_x), wrapped(x - 1, coarse_x)

            def part(at, component):
                return upper[at, pl.ds(component * coarse_z, coarse_z)]

            for axis, (in_x, in_y, in_z) in enumerate(((0, 3, 4), (3, 1, 5), (4, 5, 2))):
                along_y, along_z = part(x, in_y), part(x, in_z)
                total = part(ahead, in_x) - part(behind, in_x)
                total = total + shifted(along_y, 2, 1) - shifted(along_y, -2, 1)
                total = 0.25 * (total + shifted(along_z, 1, 0) - shifted(along_z, -1, 0))
                force[x, axis] = jnp.broadcast_to(total[:, None], (coarse_z, 2, ring)).reshape(big_z, ring)

    def rates(src, x, give):
        ahead, behind = wrapped(x + 1, big_x), wrapped(x - 1, big_x)
        half = [0.5 * src[c, x] for c in range(3)]
        u, v, w = half
        plus = [VISCOSITY - h for h in half]
        minus = [VISCOSITY + h for h in half]
        for c in range(fields):
            q = src[c, x]
            rate = plus[0] * src[c, ahead] + minus[0] * src[c, behind]
            rate = rate + plus[1] * shifted(q, 1, 1) + minus[1] * shifted(q, -1, 1)
            rate = rate + plus[2] * shifted(q, 1, 0) + minus[2] * shifted(q, -1, 0)
            rate = rate - (6.0 * VISCOSITY) * q
            if c < 3:
                rate = rate + force[x // 2, c]
            give(c, q, rate)

    forces(base)

    @pl.loop(0, big_x, unroll=unroll)
    def _(x):
        def give(c, q, rate):
            state[c, x] = q + TIME_STEP * rate

        rates(base, x, give)

    forces(state)

    @pl.loop(0, big_x, unroll=unroll)
    def _(x):
        def give(c, q, rate):
            base[c, x] = 0.75 * base[c, x] + 0.25 * (q + TIME_STEP * rate)

        rates(state, x, give)

    forces(base, last=True)

    for x in range(xs):
        def give(c, q, rate):
            moved = (q + TIME_STEP * rate)[:depth, :lanes]
            out_ref[c, :, x, :] = own_ref[c, x] * (1.0 / 3.0) + (2.0 / 3.0) * moved

        rates(base, x, give)


def step(main, edge, own, w1, bias, w2, pool, spread, nets, wides):
    fields, xs, depth, lanes = own.shape
    big_x, big_z, ring = xs * wides, depth * nets, lanes + EDGE
    coarse_x, coarse_ring = big_x // 2, pool.shape[0]
    block = fields * big_z
    part_x = math.gcd(coarse_x, max(1, 512 // block))
    stage = math.gcd(nets * wides, 8)
    batch = math.gcd(coarse_x, 8 if block < 128 else 1)
    channels, width = w2.shape[1], w2.shape[2] // 3
    return pl.pallas_call(
        functools.partial(step_kernel, nets, wides),
        out_shape=jax.ShapeDtypeStruct((fields, depth, xs, lanes), jnp.float32),
        in_specs=[pl.BlockSpec(memory_space=pl.ANY)] * 2 + [pl.BlockSpec(memory_space=pltpu.VMEM)] * 6,
        out_specs=pl.BlockSpec(memory_space=pltpu.VMEM),
        scratch_shapes=[
            pltpu.VMEM((fields, big_x, big_z, ring), jnp.float32),
            pltpu.VMEM((fields, big_x, big_z, ring), jnp.float32),
            pltpu.VMEM((part_x * block, 2 * ring), jnp.bfloat16),
            pltpu.VMEM((3, coarse_ring, coarse_x * block + 2 * max(128, block)), jnp.bfloat16),
            pltpu.VMEM((batch, coarse_ring, 3 * channels), jnp.bfloat16),
            pltpu.VMEM((coarse_x, coarse_ring, width), jnp.float32),
            pltpu.VMEM((coarse_x * width, coarse_ring), jnp.bfloat16),
            pltpu.VMEM((coarse_x, width, ring), jnp.float32),
            pltpu.VMEM((coarse_x, 3, big_z, ring), jnp.float32),
            pltpu.VMEM((stage, *main.shape[1:]), main.dtype),
            pltpu.VMEM((stage, *edge.shape[1:]), edge.dtype),
            pltpu.SemaphoreType.DMA((2,)),
        ],
        compiler_params=pltpu.CompilerParams(vmem_limit_bytes=60 * 1024 * 1024),
    )(main, edge, own, w1, bias, w2, pool, spread)


HALO = 16


def constants(lanes, big_z, fields, hidden, parts):
    ring, own, coarse_z = lanes + EDGE, lanes // 2, big_z // 2
    coarse_ring = own + 2 * HALO
    covers = np.zeros((coarse_ring, ring), np.float32)
    for m in range(coarse_ring):
        first = 2 * m if m < own + HALO else ring - 2 * (coarse_ring - m)
        covers[m, first : first + 2] = 1.0
    pool = np.concatenate([covers, covers], 1) * 0.125
    block = fields * big_z
    group = max(1, 128 // block)
    slots = 3 if group == 1 else 2 * group
    rows = np.arange(slots * block)
    slot, channel = rows // block, rows // big_z % fields
    pick1 = np.zeros((group, slots * block, 24), np.float32)
    for variant in range(group):
        for dx in range(3):
            for c in range(fields):
                here = (slot == (variant - 1) % group + dx) & (channel == c)
                pick1[variant, here, 8 * dx + c] = 1.0
    width = parts * coarse_z
    width = 64 if width <= 64 else -(-width // 128) * 128
    pick2 = np.zeros((3 * width, 24), np.float32)
    for dx in range(3):
        for s in range(parts):
            start = dx * width + s * coarse_z
            pick2[start : start + coarse_z, 8 * dx + s] = 1.0
    tile = np.tile(np.eye(hidden, dtype=np.float32), (1, coarse_z))
    return [jnp.asarray(a, jnp.bfloat16) for a in (pool, covers, pick1, pick2, tile)]


def per_device(nets, wides, narrows, fields, conv1_weight, conv1_bias, conv2_weight):
    count, depth, xs, lanes = fields.shape
    big_z = depth * nets
    hidden, parts = conv1_weight.shape[1], conv2_weight.shape[1]
    pool, spread, *picks = constants(lanes, big_z, count, hidden, parts)
    main, edge, w1, w2, own = gather(
        fields, conv1_weight.transpose(0, 2, 1), conv2_weight.transpose(1, 0, 2), picks,
        picks[1].shape[0] // 3, big_z, nets, wides, narrows,
    )
    bias = conv1_bias[None]
    return step(main, edge, own, w1, bias, w2, pool, spread, nets, wides)


def solution(mesh):
    in_specs = (P(None, "net", "wide", "narrow"), P(), P(), P())
    out_specs = P(None, "net", "wide", "narrow")
    sizes = (mesh.shape["net"], mesh.shape["wide"], mesh.shape["narrow"])
    return jax.shard_map(
        functools.partial(per_device, *sizes), mesh=mesh, in_specs=in_specs, out_specs=out_specs, check_vma=False
    )
```

```python
import functools
import math

import jax
import jax.numpy as jnp
import numpy as np
from jax import lax
from jax.experimental import pallas as pl
from jax.experimental.pallas import tpu as pltpu
from jax.sharding import PartitionSpec as P

MESH = pl.DeviceIdType.MESH
TIME_STEP = 0.2
VISCOSITY = 0.05
EDGE = 128


def joined_weights(conv1_ref, conv2_ref, pick1_ref, pick2_ref, tile_ref, w1_ref, w2_ref, big_z):
    coarse_z = big_z // 2
    f32, bf16 = jnp.float32, jnp.bfloat16
    tile = tile_ref[...]
    hidden = tile.shape[0]
    rows, columns = w1_ref.shape[2:]
    zi = lax.broadcasted_iota(jnp.int32, (rows, columns), 0) % big_z
    zo = lax.broadcasted_iota(jnp.int32, (rows, columns), 1) // hidden
    masks1 = [zi == 2 * ((zo + dz + coarse_z - 1) % coarse_z) for dz in range(3)]
    shape2 = (w2_ref.shape[1], w2_ref.shape[2])
    width = shape2[1] // 3
    zi = lax.broadcasted_iota(jnp.int32, shape2, 0) // hidden
    zo = lax.broadcasted_iota(jnp.int32, shape2, 1) % width % coarse_z
    masks2 = [zi == (zo + dz + coarse_z - 1) % coarse_z for dz in range(3)]

    def stacked(ref, dz, dy):
        pieces = []
        for dx in range(3):
            piece = ref(9 * dz + 3 * dx + dy)
            pieces += [piece, jnp.zeros((8 - piece.shape[0], hidden), f32)]
        return jnp.concatenate(pieces, axis=0).astype(bf16)

    second = conv2_ref[...].astype(f32)

    def second_tap(t):
        return jnp.concatenate([second[i, t : t + 1] for i in range(second.shape[0])], axis=0)

    def build(dy):
        total = [None] * w1_ref.shape[0]
        for dz in range(3):
            spread = jnp.dot(stacked(lambda t: conv1_ref[t].astype(f32), dz, dy), tile, preferred_element_type=f32).astype(bf16)
            for variant in range(len(total)):
                term = jnp.dot(pick1_ref[variant], spread, preferred_element_type=f32)
                term = jnp.where(masks1[dz], term, 0.0)
                total[variant] = term if dz == 0 else total[variant] + term
        for variant, value in enumerate(total):
            w1_ref[variant, dy] = value.astype(bf16)
        value = None
        for dz in range(3):
            repeated = jnp.dot(pick2_ref[...], stacked(second_tap, dz, dy), preferred_element_type=f32).astype(bf16)
            term = lax.dot_general(tile, repeated, (((0,), (1,)), ((), ())), preferred_element_type=f32)
            term = jnp.where(masks2[dz], term, 0.0)
            value = term if dz == 0 else value + term
        w2_ref[dy] = value.astype(bf16)

    return build


def gather_kernel(nets, wides, narrows, big_z, state_ref, conv1_ref, conv2_ref, pick1_ref, pick2_ref, tile_ref,
                  main_ref, edge_ref, w1_ref, w2_ref, turned_ref, own_ref, after, before, packed,
                  y_send, y_recv, main_send, main_recv, edge_send, edge_recv, local_sem):
    net, wide, narrow = lax.axis_index("net"), lax.axis_index("wide"), lax.axis_index("narrow")
    up, down = lax.rem(narrow + 1, narrows), lax.rem(narrow + narrows - 1, narrows)
    length = own_ref.shape[1]

    def device(n, w, k):
        return {"net": n, "wide": w, "narrow": k}

    def target(dn, dw):
        return device(lax.rem(net + nets - dn, nets), lax.rem(wide + wides - dw, wides), narrow)

    core = lax.rem(wide, 2)
    partner = device(net, wide + 1 - 2 * core, narrow)
    direct = [(dn, dw) for dn in range(nets) for dw in range(0, wides, 2) if (dn, dw) != (0, 0)]
    handed = [dn * wides + dw for dn in range(nets) for dw in range(1, wides, 2)]

    barrier = pltpu.get_barrier_semaphore()
    for k in (up, down):
        pl.semaphore_signal(barrier, inc=1, device_id=device(net, wide, k), device_id_type=MESH)
    for dn, dw in direct:
        pl.semaphore_signal(barrier, inc=1, device_id=target(dn, dw), device_id_type=MESH)
    pl.semaphore_signal(barrier, inc=1, device_id=partner, device_id_type=MESH)
    for f in range(state_ref.shape[0]):
        for x in range(state_ref.shape[2]):
            turned_ref[f, x] = state_ref[f, :, x, :]
    own_ref[...] = turned_ref[...].reshape(own_ref.shape).astype(own_ref.dtype)
    pl.semaphore_wait(barrier, 3 + len(direct))

    def remote(src, dst, send, recv, where):
        return pltpu.make_async_remote_copy(
            src_ref=src, dst_ref=dst, send_sem=send, recv_sem=recv, device_id=where, device_id_type=MESH
        )

    to_down = remote(own_ref.at[:, pl.ds(0, EDGE)], after, y_send.at[0], y_recv.at[0], device(net, wide, down))
    to_up = remote(own_ref.at[:, pl.ds(length - EDGE, EDGE)], before, y_send.at[1], y_recv.at[1], device(net, wide, up))
    to_down.start()
    to_up.start()
    def hand_on(src, ref, dn, dw, send, recv):
        slot = dn * wides + lax.rem(dw + wides - 1 + 2 * core, wides)
        return remote(src, ref.at[slot], send.at[slot], recv.at[slot], partner)

    mains, sent = [], []
    for dn, dw in direct:
        slot = dn * wides + dw
        mains.append(remote(own_ref, main_ref.at[slot], main_send.at[slot], main_recv.at[slot], target(dn, dw)))
        mains[-1].start()
    sent.append(hand_on(own_ref, main_ref, 0, 0, main_send, main_recv))
    sent[-1].start()
    own_main = pltpu.make_async_copy(own_ref, main_ref.at[0], local_sem.at[0])
    own_main.start()
    build = joined_weights(conv1_ref, conv2_ref, pick1_ref, pick2_ref, tile_ref, w1_ref, w2_ref, big_z)
    build(0)
    to_down.wait()
    to_up.wait()
    lane = lax.broadcasted_iota(jnp.int32, after.shape, 1)
    packed[...] = jnp.where(
        lane < EDGE // 2, after[...].astype(jnp.float32), before[...].astype(jnp.float32)
    ).astype(packed.dtype)
    edges = []
    for dn, dw in direct:
        slot = dn * wides + dw
        edges.append(remote(packed, edge_ref.at[slot], edge_send.at[slot], edge_recv.at[slot], target(dn, dw)))
        edges[-1].start()
    sent.append(hand_on(packed, edge_ref, 0, 0, edge_send, edge_recv))
    sent[-1].start()
    own_edge = pltpu.make_async_copy(packed, edge_ref.at[0], local_sem.at[1])
    own_edge.start()
    build(1)
    for copies, ref, send, recv in ((mains, main_ref, main_send, main_recv), (edges, edge_ref, edge_send, edge_recv)):
        for copy, (dn, dw) in zip(copies, direct):
            copy.wait_recv()
            sent.append(hand_on(ref.at[dn * wides + dw], ref, dn, dw, send, recv))
            sent[-1].start()
        if ref is main_ref:
            build(2)
    for copy in mains + edges + sent:
        copy.wait_send()
    for slot in handed:
        remote(main_ref.at[slot], main_ref.at[slot], main_send.at[slot], main_recv.at[slot], partner).wait_recv()
        remote(edge_ref.at[slot], edge_ref.at[slot], edge_send.at[slot], edge_recv.at[slot], partner).wait_recv()
    own_main.wait()
    own_edge.wait()


def gather(own, conv1, conv2, picks, width, big_z, nets, wides, narrows):
    count, depth, xs, length = own.shape
    rows = count * depth * xs
    travel = jnp.bfloat16
    columns = picks[2].shape[1]
    slots = nets * wides
    return pl.pallas_call(
        functools.partial(gather_kernel, nets, wides, narrows, big_z),
        out_shape=[
            jax.ShapeDtypeStruct((slots, rows, length), travel),
            jax.ShapeDtypeStruct((slots, rows, EDGE), travel),
            jax.ShapeDtypeStruct((picks[0].shape[0], 3, picks[0].shape[1], columns), jnp.bfloat16),
            jax.ShapeDtypeStruct((3, columns, 3 * width), jnp.bfloat16),
            jax.ShapeDtypeStruct((count, xs, depth, length), jnp.float32),
        ],
        in_specs=[pl.BlockSpec(memory_space=pltpu.VMEM)] * 6,
        out_specs=[pl.BlockSpec(memory_space=pl.ANY)] * 2 + [pl.BlockSpec(memory_space=pltpu.VMEM)] * 3,
        scratch_shapes=[
            pltpu.VMEM((rows, length), travel),
            pltpu.VMEM((rows, EDGE), travel),
            pltpu.VMEM((rows, EDGE), travel),
            pltpu.VMEM((rows, EDGE), travel),
            pltpu.SemaphoreType.DMA((2,)),
            pltpu.SemaphoreType.DMA((2,)),
            pltpu.SemaphoreType.DMA((slots,)),
            pltpu.SemaphoreType.DMA((slots,)),
            pltpu.SemaphoreType.DMA((slots,)),
            pltpu.SemaphoreType.DMA((slots,)),
            pltpu.SemaphoreType.DMA((2,)),
        ],
        compiler_params=pltpu.CompilerParams(
            collective_id=0, has_side_effects=True, vmem_limit_bytes=60 * 1024 * 1024
        ),
    )(own, conv1, conv2, *picks)


def shifted(values, offset, axis):
    return pltpu.roll(values, (-offset) % values.shape[axis], axis)


def two_parts(values):
    high = values.astype(jnp.bfloat16)
    low = (values - high.astype(jnp.float32)).astype(jnp.bfloat16)
    return high, low


def gelu(x):
    inner = x * (0.7978845608028654 + 0.035677408136300125 * (x * x))
    half = 0.5 * x
    return half + half * jnp.tanh(inner)


def step_kernel(nets, wides, main_ref, edge_ref, own_ref, w1_ref, bias_ref, w2_ref, pool_ref, spread_ref,
                out_ref, base, state, thin, taps, wide_hidden, partial, turned, upper, force, mains, edges, arrived):
    fields, xs, depth, lanes = own_ref.shape
    big_x, big_z, ring = base.shape[1:]
    coarse_x, coarse_z = big_x // 2, big_z // 2
    coarse_ring = pool_ref.shape[0]
    block = fields * big_z
    part_x = thin.shape[0] // block
    stage = mains.shape[0]
    unroll = 2 if big_z <= 16 else 1
    variants, window = w1_ref.shape[0], w1_ref.shape[2]
    pad = (taps.shape[2] - coarse_x * block) // 2
    channels = w2_ref.shape[1]
    width = w2_ref.shape[2] // 3
    batch = wide_hidden.shape[0]
    together = max(1, 128 // width)
    bias = jnp.concatenate([bias_ref[...]] * coarse_z, axis=1)

    for begin in range(0, nets * wides, stage):
        copies = [
            pltpu.make_async_copy(main_ref.at[pl.ds(begin, stage)], mains, arrived.at[0]),
            pltpu.make_async_copy(edge_ref.at[pl.ds(begin, stage)], edges, arrived.at[1]),
        ]
        for copy in copies:
            copy.start()
        for copy in copies:
            copy.wait()
        for i in range(stage):
            dn, dw = divmod(begin + i, wides)
            x_at, z_at = pl.ds(dw * xs, xs), pl.ds(dn * depth, depth)
            if begin + i == 0:
                base[:, x_at, z_at, pl.ds(0, lanes)] = own_ref[...]
            else:
                base[:, x_at, z_at, pl.ds(0, lanes)] = (
                    mains[i].astype(jnp.float32).reshape(fields, xs, depth, lanes)
                )
            base[:, x_at, z_at, pl.ds(lanes, EDGE)] = (
                edges[i].astype(jnp.float32).reshape(fields, xs, depth, EDGE)
            )

    def each(count, body):
        if count == 1:
            body(0)
        else:
            pl.loop(0, count)(body)

    def wrapped(i, size):
        return (i + size) % size if isinstance(i, int) else lax.rem(i + size, size)

    def forces(src, last=False):
        own_x = xs // 2
        whole = batch < coarse_x or not last
        inner = [x for x in range(coarse_x) if whole or (x + 2) % coarse_x < own_x + 4]
        outer = [x for x in range(coarse_x) if whole or (x + 1) % coarse_x < own_x + 2]

        @functools.partial(each, coarse_x // part_x)
        def _(turn):
            chunk = turn * part_x

            @pl.loop(0, part_x, unroll=unroll)
            def _(i):
                x = chunk + i
                for c in range(fields):
                    both = src[c, 2 * x] + src[c, 2 * x + 1]
                    both = both + shifted(both, 1, 0)
                    high, low = two_parts(both)
                    at = pl.ds(pl.multiple_of(i * block + c * big_z, big_z), big_z)
                    thin[at, pl.ds(0, ring)] = high
                    thin[at, pl.ds(ring, ring)] = low

            coarse = lax.dot_general(
                pool_ref[...], thin[...], (((1,), (1,)), ((), ())), preferred_element_type=jnp.float32
            )
            for dy in range(3):
                moved = (coarse if dy == 1 else shifted(coarse, dy - 1, 0)).astype(jnp.bfloat16)
                at = pl.multiple_of(pad + chunk * block, 128)
                taps[dy, :, pl.ds(at, part_x * block)] = moved

        span = coarse_x * block
        taps[:, :, pl.ds(0, pad)] = taps[:, :, pl.ds(span, pad)]
        taps[:, :, pl.ds(pad + span, pad)] = taps[:, :, pl.ds(pad, pad)]

        if batch < coarse_x:
            partial[...] = jnp.zeros_like(partial)

        @functools.partial(each, coarse_x // batch)
        def _(turn):
            begin = turn * batch
            for variant in range(variants):
                mine = [x for x in range(variant, batch, variants) if batch < coarse_x or x in inner]
                rows = []
                for x in mine:
                    at = pl.multiple_of(begin * block + (pad + (x - 1) * block) // 128 * 128, 128)
                    rows.append(jnp.concatenate([taps[dy, :, pl.ds(at, window)] for dy in range(3)], axis=1))
                around = jnp.concatenate(rows, axis=0)
                weight = w1_ref[variant].reshape(3 * window, channels)
                hidden = jnp.dot(around, weight, preferred_element_type=jnp.float32) + bias
                hidden = gelu(hidden)
                for i, x in enumerate(mine):
                    here = hidden[i * coarse_ring : (i + 1) * coarse_ring]
                    for dy in range(3):
                        moved = (here if dy == 1 else shifted(here, dy - 1, 0)).astype(jnp.bfloat16)
                        wide_hidden[x, :, pl.ds(dy * channels, channels)] = moved
            used = range(batch) if batch < coarse_x else inner
            found = jnp.dot(
                jnp.concatenate([wide_hidden[x] for x in used], axis=0),
                w2_ref[...].reshape(3 * channels, 3 * width),
                preferred_element_type=jnp.float32,
            )
            found = found.reshape(len(used), coarse_ring, 3 * width)
            for i in range(batch):
                if batch == coarse_x:
                    if i in outer:
                        left, here, right = [inner.index((i + d) % coarse_x) for d in (-1, 0, 1)]
                        total = found[left, :, :width] + found[here, :, width : 2 * width]
                        partial[i] = total + found[right, :, 2 * width :]
                else:
                    for dx in range(3):
                        partial[wrapped(begin + i + 1 - dx, coarse_x)] += found[i, :, dx * width : (dx + 1) * width]

        def turn_over(x):
            totals = [partial[x + i] for i in range(together)]
            total = jnp.concatenate(totals, axis=1) if together > 1 else totals[0]
            at = x * width if isinstance(x, int) else pl.multiple_of(x * width, width)
            turned[pl.ds(at, together * width), :] = total.T.astype(jnp.bfloat16)

        if batch == coarse_x:
            for x in range(0, coarse_x, together):
                if any(x + i in outer for i in range(together)):
                    turn_over(x)
        else:
            pl.loop(0, coarse_x // together)(lambda i: turn_over(i * together))

        @functools.partial(each, coarse_x // batch)
        def _(turn):
            begin = turn * batch
            at = pl.multiple_of(begin * width, batch * width)
            fine = jnp.dot(
                turned[pl.ds(at, batch * width), :], spread_ref[...], preferred_element_type=jnp.float32
            )
            upper[pl.ds(begin, batch)] = fine.reshape(batch, width, ring)

        @pl.loop(0, own_x if last else coarse_x, unroll=unroll)
        def _(x):
            ahead, behind = wrapped(x + 1, coarse_x), wrapped(x - 1, coarse_x)

            def part(at, component):
                return upper[at, pl.ds(component * coarse_z, coarse_z)]

            for axis, (in_x, in_y, in_z) in enumerate(((0, 3, 4), (3, 1, 5), (4, 5, 2))):
                along_y, along_z = part(x, in_y), part(x, in_z)
                total = part(ahead, in_x) - part(behind, in_x)
                total = total + shifted(along_y, 2, 1) - shifted(along_y, -2, 1)
                total = 0.25 * (total + shifted(along_z, 1, 0) - shifted(along_z, -1, 0))
                force[x, axis] = jnp.broadcast_to(total[:, None], (coarse_z, 2, ring)).reshape(big_z, ring)

    def rates(src, x, give):
        ahead, behind = wrapped(x + 1, big_x), wrapped(x - 1, big_x)
        half = [0.5 * src[c, x] for c in range(3)]
        u, v, w = half
        plus = [VISCOSITY - h for h in half]
        minus = [VISCOSITY + h for h in half]
        for c in range(fields):
            q = src[c, x]
            rate = plus[0] * src[c, ahead] + minus[0] * src[c, behind]
            rate = rate + plus[1] * shifted(q, 1, 1) + minus[1] * shifted(q, -1, 1)
            rate = rate + plus[2] * shifted(q, 1, 0) + minus[2] * shifted(q, -1, 0)
            rate = rate - (6.0 * VISCOSITY) * q
            if c < 3:
                rate = rate + force[x // 2, c]
            give(c, q, rate)

    forces(base)

    @pl.loop(0, big_x, unroll=2 * unroll if unroll > 1 else 1)
    def _(x):
        def give(c, q, rate):
            state[c, x] = q + TIME_STEP * rate

        rates(base, x, give)

    forces(state)

    @pl.loop(0, big_x, unroll=2 * unroll if unroll > 1 else 1)
    def _(x):
        def give(c, q, rate):
            base[c, x] = 0.75 * base[c, x] + 0.25 * (q + TIME_STEP * rate)

        rates(state, x, give)

    forces(base, last=True)

    for x in range(xs):
        def give(c, q, rate):
            moved = (q + TIME_STEP * rate)[:depth, :lanes]
            out_ref[c, :, x, :] = own_ref[c, x] * (1.0 / 3.0) + (2.0 / 3.0) * moved

        rates(base, x, give)


def step(main, edge, own, w1, bias, w2, pool, spread, nets, wides):
    fields, xs, depth, lanes = own.shape
    big_x, big_z, ring = xs * wides, depth * nets, lanes + EDGE
    coarse_x, coarse_ring = big_x // 2, pool.shape[0]
    block = fields * big_z
    part_x = math.gcd(coarse_x, max(1, 512 // block))
    stage = math.gcd(nets * wides, 8)
    batch = math.gcd(coarse_x, 8 if block < 128 else 1)
    channels, width = w2.shape[1], w2.shape[2] // 3
    return pl.pallas_call(
        functools.partial(step_kernel, nets, wides),
        out_shape=jax.ShapeDtypeStruct((fields, depth, xs, lanes), jnp.float32),
        in_specs=[pl.BlockSpec(memory_space=pl.ANY)] * 2 + [pl.BlockSpec(memory_space=pltpu.VMEM)] * 6,
        out_specs=pl.BlockSpec(memory_space=pltpu.VMEM),
        scratch_shapes=[
            pltpu.VMEM((fields, big_x, big_z, ring), jnp.float32),
            pltpu.VMEM((fields, big_x, big_z, ring), jnp.float32),
            pltpu.VMEM((part_x * block, 2 * ring), jnp.bfloat16),
            pltpu.VMEM((3, coarse_ring, coarse_x * block + 2 * max(128, block)), jnp.bfloat16),
            pltpu.VMEM((batch, coarse_ring, 3 * channels), jnp.bfloat16),
            pltpu.VMEM((coarse_x, coarse_ring, width), jnp.float32),
            pltpu.VMEM((coarse_x * width, coarse_ring), jnp.bfloat16),
            pltpu.VMEM((coarse_x, width, ring), jnp.float32),
            pltpu.VMEM((coarse_x, 3, big_z, ring), jnp.float32),
            pltpu.VMEM((stage, *main.shape[1:]), main.dtype),
            pltpu.VMEM((stage, *edge.shape[1:]), edge.dtype),
            pltpu.SemaphoreType.DMA((2,)),
        ],
        compiler_params=pltpu.CompilerParams(vmem_limit_bytes=60 * 1024 * 1024),
    )(main, edge, own, w1, bias, w2, pool, spread)


HALO = 16


def constants(lanes, big_z, fields, hidden, parts):
    ring, own, coarse_z = lanes + EDGE, lanes // 2, big_z // 2
    coarse_ring = own + 2 * HALO
    covers = np.zeros((coarse_ring, ring), np.float32)
    for m in range(coarse_ring):
        first = 2 * m if m < own + HALO else ring - 2 * (coarse_ring - m)
        covers[m, first : first + 2] = 1.0
    pool = np.concatenate([covers, covers], 1) * 0.125
    block = fields * big_z
    group = max(1, 128 // block)
    slots = 3 if group == 1 else 2 * group
    rows = np.arange(slots * block)
    slot, channel = rows // block, rows // big_z % fields
    pick1 = np.zeros((group, slots * block, 24), np.float32)
    for variant in range(group):
        for dx in range(3):
            for c in range(fields):
                here = (slot == (variant - 1) % group + dx) & (channel == c)
                pick1[variant, here, 8 * dx + c] = 1.0
    width = parts * coarse_z
    width = 64 if width <= 64 else -(-width // 128) * 128
    pick2 = np.zeros((3 * width, 24), np.float32)
    for dx in range(3):
        for s in range(parts):
            start = dx * width + s * coarse_z
            pick2[start : start + coarse_z, 8 * dx + s] = 1.0
    tile = np.tile(np.eye(hidden, dtype=np.float32), (1, coarse_z))
    return [jnp.asarray(a, jnp.bfloat16) for a in (pool, covers, pick1, pick2, tile)]


def per_device(nets, wides, narrows, fields, conv1_weight, conv1_bias, conv2_weight):
    count, depth, xs, lanes = fields.shape
    big_z = depth * nets
    hidden, parts = conv1_weight.shape[1], conv2_weight.shape[1]
    pool, spread, *picks = constants(lanes, big_z, count, hidden, parts)
    main, edge, w1, w2, own = gather(
        fields, conv1_weight.transpose(0, 2, 1), conv2_weight.transpose(1, 0, 2), picks,
        picks[1].shape[0] // 3, big_z, nets, wides, narrows,
    )
    bias = conv1_bias[None]
    return step(main, edge, own, w1, bias, w2, pool, spread, nets, wides)


def solution(mesh):
    in_specs = (P(None, "net", "wide", "narrow"), P(), P(), P())
    out_specs = P(None, "net", "wide", "narrow")
    sizes = (mesh.shape["net"], mesh.shape["wide"], mesh.shape["narrow"])
    return jax.shard_map(
        functools.partial(per_device, *sizes), mesh=mesh, in_specs=in_specs, out_specs=out_specs, check_vma=False
    )
```
